32 devices in a mesh: dev: 32 (over z, y, x, core).
Axes of the slice: x: 2, y: 2, z: 4, core: 2. Of those that a mesh axis runs over, the one named last changes fastest.
Arguments:
- cotangent: bfloat16 [8192, 2048], P('dev'), may hold values from -6 to 6
- hot_table: bfloat16 [2048, 128], replicated, may hold values from -6 to 6
- cold_table: float32 [65536, 128], P('dev'), may hold values from -6 to 6
- cold_m: float32 [65536, 128], P('dev'), may hold values from -0.75 to 0.75
- cold_v: float32 [65536, 128], P('dev'), may hold values from 0.0001 to 0.01
- cross_down: bfloat16 [2048, 512], replicated, may hold values from -0.125 to 0.125
- cross_up: bfloat16 [512, 2048], replicated, may hold values from -0.25 to 0.25
- cross_bias: float32 [2048], replicated, may hold values from -6 to 6
- dense_master: float32 [2048, 1024], P('dev'), may hold values from -0.4375 to 0.4375
- dense_m: float32 [2048, 1024], P('dev'), may hold values from -6 to 6
- dense_v: float32 [2048, 1024], P('dev'), may hold values from 1 to 30
- hot_ids: int32 [8192, 16], P('dev'), may hold values from 0 to 2047
- lookup_slot: int32 [8192, 16], P('dev'), may hold values from -1 to 3071, as said below
- fetch_rows: int32 [32, 32, 96], P('dev'), may hold values from 0 to 2047, as said below
Outputs:
- hot_grad: float32 [2048, 128], replicated
- bias_grad: float32 [2048], replicated
- cold_new: float32 [65536, 128], P('dev')
- cold_m_new: float32 [65536, 128], P('dev')
- cold_v_new: float32 [65536, 128], P('dev')
- master_new: float32 [2048, 1024], P('dev')
- dense_m_new: float32 [2048, 1024], P('dev')
- dense_v_new: float32 [2048, 1024], P('dev')
- new_weights: bfloat16 [2048, 1024], replicated
The draws below stay inside these ranges and needn't reach their ends.
Inputs may be any that keep to these rules, and one draw needn't show every extreme that they name: `lookup_slot`: -1 marks a hot lookup; any other value o * 96 + s reads slot s of the list that the lookup's device sends to owner o. For each device and owner the slots read are 0 to c - 1 for some c of at most 96, each read by exactly one lookup of that device; every device reads 96 slots from some owner, and some owner is read 96 slots by every device. `fetch_rows`: slots that no lookup reads still name rows.
All inputs are finite; a program needn't handle non-finite values.
Results may differ from the reference program's by a relative error of at most 0.0055.
Values may be sent and summed in bfloat16 or wider, within the bound.
No kernel may reach another device: no remote copies, remote signals or barrier semaphores. Data moves between devices by JAX's collectives and lax.ppermute only.
A program may use at most 128 MiB of HBM per device.

```python
import math
import jax
import jax.numpy as jnp
from jax import lax

E = 128
F = 16
RANK = 512
HOT = 2048
SLAB = 2048
B_DEV = 256
CROSS = 2048
BATCH = 8192
MEAN_PAIR = 32
CAP = 96
COLD_ROWS = 65536
N_DEV = 32


def plan_counts(key):
    owner_order = jax.random.permutation(jax.random.fold_in(key, 11), N_DEV)
    owner_rank = jnp.zeros((N_DEV,), jnp.int32).at[owner_order].set(jnp.arange(N_DEV, dtype=jnp.int32))
    heavy_owner = owner_rank < N_DEV // 8
    heavy_counts = CAP - jax.random.randint(jax.random.fold_in(key, 12), (N_DEV, N_DEV), 0, MEAN_PAIR)
    light_counts = jax.random.randint(jax.random.fold_in(key, 13), (N_DEV, N_DEV), 0, 2 * MEAN_PAIR + 1)
    counts = jnp.where(heavy_owner[None, :], heavy_counts, light_counts).astype(jnp.int32)
    counts = counts.at[:, owner_order[0]].set(CAP)
    counts = counts.at[0, N_DEV - 1].set(CAP)
    return counts


def draw_lookup_slot(key, part):
    counts = plan_counts(key)
    lookups = B_DEV * F

    def one_device(device_counts, device_key):
        slot_ends = jnp.cumsum(device_counts).astype(jnp.int32)
        starts = slot_ends - device_counts
        places = jnp.arange(lookups, dtype=jnp.int32)
        owners = jnp.minimum(jnp.searchsorted(slot_ends, places, side='right'), N_DEV - 1).astype(jnp.int32)
        slot_index = places - starts[owners]
        slot_codes = jnp.where(places < slot_ends[-1], owners * CAP + slot_index, -1).astype(jnp.int32)
        shuffle = jax.random.permutation(device_key, lookups)
        return jnp.zeros((lookups,), jnp.int32).at[shuffle].set(slot_codes)
    device_keys = jax.random.split(jax.random.fold_in(key, 14), N_DEV)
    placed = jax.vmap(one_device)(counts, device_keys)
    return placed.reshape(N_DEV * B_DEV, F).astype(jnp.int32)


def draw_fetch_rows(key, part):
    return jax.random.randint(jax.random.fold_in(key, 15), (N_DEV, N_DEV, CAP), 0, SLAB).astype(jnp.int32)


def set_ends(drawn, stream_key, low, top_value):
    shape = drawn.shape
    place = [jax.random.randint(jax.random.fold_in(stream_key, axis), (), 0, shape[axis]) for axis in range(len(shape))]
    drawn = drawn.at[tuple(place)].set(low)
    longest = shape.index(max(shape))
    place[longest] = (place[longest] + 1) % shape[longest]
    return drawn.at[tuple(place)].set(top_value)


def level_of(rng, dims, cuts, least, high):
    factor_of = 1.0
    for axis_at, shards_of in cuts:
        draws = jax.random.uniform(jax.random.fold_in(jax.random.fold_in(rng, 6), axis_at), (shards_of,), jnp.float32, least / len(cuts), high / len(cuts))
        factor_of = factor_of * jnp.repeat(jnp.exp(draws), dims[axis_at] // shards_of).reshape((-1,) + (1,) * (len(dims) - 1 - axis_at))
    return factor_of


def centred(stream_key, dims, deviation, most, shards=(), kind=jnp.bfloat16):
    values = jax.random.normal(stream_key, dims, jnp.float32) * deviation
    if len(shards) > 0:
        values = level_of(stream_key, dims, shards, -0.22, 0.18) * values
    return jnp.clip(values, min=-most, max=most).astype(kind)


def setup_inputs(seed: int = 0) -> dict:
    key_list = jax.random.split(jax.random.key(seed), 15)
    cotangent = centred(key_list[0], (BATCH, CROSS), 1.0, 6.0, ((0, 32),))
    hot_table = centred(key_list[1], (HOT, E), 1.0, 6.0)
    cold_table = centred(key_list[2], (COLD_ROWS, E), 1.0, 6.0, ((0, 32),), jnp.float32)
    cold_m = centred(key_list[3], (COLD_ROWS, E), 0.05, 0.75, ((0, 32),), jnp.float32)
    cold_v = jnp.clip(jnp.exp(math.log(0.01) - 4.6051702 * jax.random.uniform(key_list[4], (COLD_ROWS, E), jnp.float32) ** level_of(key_list[4], (COLD_ROWS, E), ((0, 32),), -0.2, 0.2)), 0.0001, 0.01)
    cross_down = centred(key_list[5], (CROSS, RANK), CROSS ** -0.5, 0.125)
    cross_up = centred(key_list[6], (RANK, CROSS), RANK ** -0.5, 0.25)
    cross_bias = centred(key_list[7], (CROSS,), 0.5, 6.0, (), jnp.float32)
    dense_master = centred(key_list[8], (CROSS, 2 * RANK), 0.03, 0.4375, ((0, 32),), jnp.float32)
    dense_m = centred(key_list[9], (CROSS, 2 * RANK), 0.5, 6.0, ((0, 32),), jnp.float32)
    dense_v = jnp.clip(jnp.exp(math.log(30.0) - 3.4011974 * jax.random.uniform(key_list[10], (CROSS, 2 * RANK), jnp.float32) ** level_of(key_list[10], (CROSS, 2 * RANK), ((0, 32),), -0.2, 0.2)), 1.0, 30.0)
    hot_ids = set_ends(jax.random.randint(key_list[11], (BATCH, F), 0, HOT), jax.random.fold_in(key_list[11], 1), 0, HOT - 1).astype(jnp.int32)
    lookup_slot = draw_lookup_slot(jax.random.fold_in(key_list[14], 71), 0)
    fetch_rows = draw_fetch_rows(jax.random.fold_in(key_list[14], 71), 0)
    return dict(cotangent=cotangent, hot_table=hot_table, cold_table=cold_table, cold_m=cold_m, cold_v=cold_v, cross_down=cross_down, cross_up=cross_up, cross_bias=cross_bias, dense_master=dense_master, dense_m=dense_m, dense_v=dense_v, hot_ids=hot_ids, lookup_slot=lookup_slot, fetch_rows=fetch_rows)


first_decay = 0.9
second_decay = 0.999
adam_epsilon = 1e-08
learn_rate = 0.01
first_fix = 1.0 - (0.9 ** 10) ** 10
second_fix = 1.0 - (0.999 ** 10) ** 10

def adam_update(params, moment_one, moment_two, gradient):
    moment_one = first_decay * moment_one + (1.0 - first_decay) * gradient
    moment_two = second_decay * moment_two + (1.0 - second_decay) * gradient * gradient
    params = params - learn_rate * (moment_one / first_fix) / (jnp.sqrt(moment_two / second_fix) + adam_epsilon)
    return (params, moment_one, moment_two)

def reference(cotangent, hot_table, cold_table, cold_m, cold_v, cross_down, cross_up, cross_bias, dense_master, dense_m, dense_v, hot_ids, lookup_slot, fetch_rows):
    cold_half = cold_table.astype(jnp.bfloat16)
    owner_base = (jnp.arange(N_DEV, dtype=jnp.int32) * SLAB)[:, None]

    def per_device(totals, requester):
        hot_sum, bias_sum, dense_sum, cold_sum = totals
        first_row = (requester * B_DEV).astype(jnp.int32)
        grad_out = lax.dynamic_slice_in_dim(cotangent, first_row, B_DEV, 0)
        hot_index = lax.dynamic_slice_in_dim(hot_ids, first_row, B_DEV, 0)
        slot_code = lax.dynamic_slice_in_dim(lookup_slot, first_row, B_DEV, 0)
        requests = lax.dynamic_index_in_dim(fetch_rows, requester, 0, keepdims=False)
        global_rows = (owner_base + requests).reshape(-1).astype(jnp.int32)
        fetched = cold_half[global_rows]
        is_hot = slot_code < 0
        cold_pos = jnp.maximum(slot_code, 0)
        picked = jnp.where(is_hot[..., None], hot_table[hot_index], fetched[cold_pos])
        inputs = picked.reshape(B_DEV, CROSS)
        latent = jnp.dot(inputs, cross_down, preferred_element_type=jnp.float32).astype(jnp.bfloat16)
        mixing = jnp.dot(latent, cross_up, preferred_element_type=jnp.float32) + cross_bias
        grad_f32 = grad_out.astype(jnp.float32)
        grad_mix = (grad_f32 * inputs.astype(jnp.float32)).astype(jnp.bfloat16)
        grad_latent = jnp.dot(grad_mix, cross_up.T, preferred_element_type=jnp.float32).astype(jnp.bfloat16)
        grad_input = grad_f32 * (mixing + 1.0) + jnp.dot(grad_latent, cross_down.T, preferred_element_type=jnp.float32)
        per_lookup = grad_input.reshape(B_DEV * F, E)
        hot_target = jnp.where(is_hot, hot_index, HOT).reshape(-1)
        hot_sum = hot_sum.at[hot_target].add(per_lookup, mode='drop')
        cold_target = jnp.where(is_hot, COLD_ROWS, global_rows[cold_pos]).reshape(-1)
        cold_sum = cold_sum.at[cold_target].add(per_lookup, mode='drop')
        bias_sum = bias_sum + lax.optimization_barrier(jnp.sum(grad_mix.astype(jnp.float32), axis=0))
        down_part = jnp.dot(inputs.T, grad_latent, preferred_element_type=jnp.float32)
        up_part = jnp.dot(grad_mix.T, latent, preferred_element_type=jnp.float32)
        dense_sum = dense_sum + jnp.concatenate([down_part, up_part], axis=1)
        return ((hot_sum, bias_sum, dense_sum, cold_sum), None)
    start_totals = (jnp.zeros((HOT, E), jnp.float32), jnp.zeros((CROSS,), jnp.float32), jnp.zeros((CROSS, 2 * RANK), jnp.float32), jnp.zeros((COLD_ROWS, E), jnp.float32))
    totals, unused = lax.scan(per_device, start_totals, jnp.arange(N_DEV, dtype=jnp.int32))
    hot_sum, bias_sum, dense_sum, cold_sum = totals
    scale_mean = 1.0 / N_DEV
    hot_grad = hot_sum * scale_mean
    bias_grad = bias_sum * scale_mean
    cold_new, cold_m_new, cold_v_new = adam_update(cold_table, cold_m, cold_v, cold_sum * scale_mean)
    master_new, dense_m_new, dense_v_new = adam_update(dense_master, dense_m, dense_v, dense_sum * scale_mean)
    new_weights = master_new.astype(jnp.bfloat16)
    return (hot_grad, bias_grad, cold_new, cold_m_new, cold_v_new, master_new, dense_m_new, dense_v_new, new_weights)
```

```python
import functools

import jax
import jax.numpy as jnp
from jax import lax
from jax.experimental import pallas as pl
from jax.experimental.pallas import tpu as pltpu
from jax.sharding import PartitionSpec as P

first_decay = 0.9
second_decay = 0.999
adam_epsilon = 1e-08
learn_rate = 0.01
first_fix = 1.0 - (0.9**10) ** 10
second_fix = 1.0 - (0.999**10) ** 10

LANES = 128
f32 = jnp.float32
bf16 = jnp.bfloat16


def adam_update(params, moment_one, moment_two, gradient):
    moment_one = first_decay * moment_one + (1.0 - first_decay) * gradient
    moment_two = second_decay * moment_two + (1.0 - second_decay) * gradient * gradient
    params = params - learn_rate * (moment_one / first_fix) / (
        jnp.sqrt(moment_two / second_fix) + adam_epsilon
    )
    return (params, moment_one, moment_two)


def call(kernel, outs, args, flops, name, smem=(), scratch=(), vmem=48 << 20):
    specs = [
        pl.BlockSpec(memory_space=pltpu.SMEM if i in smem else pltpu.VMEM)
        for i in range(len(args))
    ]
    moved = sum(a.size * a.dtype.itemsize for a in list(args) + list(outs))
    return pl.pallas_call(
        kernel,
        out_shape=outs,
        in_specs=specs,
        out_specs=[pl.BlockSpec(memory_space=pltpu.VMEM)] * len(outs),
        scratch_shapes=list(scratch),
        compiler_params=pltpu.CompilerParams(vmem_limit_bytes=vmem),
        cost_estimate=pl.CostEstimate(flops=flops, bytes_accessed=moved, transcendentals=0),
        name=name,
    )(*args)


def one_hot(mask):
    return jnp.where(mask, 1.0, 0.0).astype(bf16)


def owner_pick_kernel(req_ref, table_ref, out_ref, half):
    half[...] = table_ref[...].astype(bf16)
    rows = table_ref.shape[0]
    lists = req_ref.shape[0]
    columns = jnp.transpose(req_ref[...])
    step = 4 if lists % 4 == 0 else 1
    for first in range(0, lists, step):
        parts = []
        for i in range(first, first + step):
            spread = columns[:, i : i + 1]
            parts.append(
                one_hot(spread == lax.broadcasted_iota(jnp.int32, (LANES, rows), 1))
            )
        hot = jnp.concatenate(parts, axis=0)
        out_ref[first * LANES : (first + step) * LANES, :] = jnp.dot(
            hot, half[...], preferred_element_type=f32
        ).astype(bf16)


def hot_pick_kernel(ids_ref, slot_ref, table_ref, out_ref):
    samples, fields = ids_ref.shape
    rows, width = table_ref.shape
    index = jnp.where(slot_ref[...] < 0, ids_ref[...], -1)
    for f in range(fields):
        hot = one_hot(
            index[:, f : f + 1] == lax.broadcasted_iota(jnp.int32, (samples, rows), 1)
        )
        out_ref[:, f * width : (f + 1) * width] = jnp.dot(
            hot, table_ref[...], preferred_element_type=f32
        ).astype(bf16)


def forward_kernel(
    side_ref,
    slot_ref,
    fetched_ref,
    hot_ref,
    cot_ref,
    down_ref,
    up_ref,
    latent_ref,
    grad_latent_ref,
    bias_ref,
    keep_down_ref,
    send_down_ref,
    keep_up_ref,
    send_up_ref,
    x0,
    gm,
):
    samples, fields = slot_ref.shape
    slots, width = fetched_ref.shape
    index = slot_ref[...]
    for f in range(fields):
        cols = slice(f * width, (f + 1) * width)
        hot = one_hot(
            index[:, f : f + 1] == lax.broadcasted_iota(jnp.int32, (samples, slots), 1)
        )
        cold = jnp.dot(hot, fetched_ref[...], preferred_element_type=f32)
        picked = (cold + hot_ref[:, cols].astype(f32)).astype(bf16)
        x0[:, cols] = picked
        mix = cot_ref[:, cols].astype(f32) * picked.astype(f32)
        mix = mix.astype(bf16)
        gm[:, cols] = mix
        bias_ref[:, cols] = jnp.sum(mix.astype(f32), axis=0, keepdims=True)
    latent = jnp.dot(x0[...], down_ref[...], preferred_element_type=f32).astype(bf16)
    latent_ref[...] = latent
    grad_latent = lax.dot_general(
        gm[...], up_ref[...], (((1,), (1,)), ((), ())), preferred_element_type=f32
    ).astype(bf16)
    grad_latent_ref[...] = grad_latent
    chips, shard, _ = keep_down_ref.shape
    side = side_ref[0]
    block = max(2 * shard, 256)
    for keep_ref, send_ref, left, right in (
        (keep_down_ref, send_down_ref, x0, grad_latent),
        (keep_up_ref, send_up_ref, gm, latent),
    ):
        for first in range(0, chips * 2 * shard, block):
            part = lax.dot_general(
                left[:, first : first + block],
                right,
                (((0,), (0,)), ((), ())),
                preferred_element_type=f32,
            )
            for j in range(block // (2 * shard)):
                one = part[2 * j * shard : (2 * j + 1) * shard]
                two = part[(2 * j + 1) * shard : (2 * j + 2) * shard]
                at = first // (2 * shard) + j
                keep_ref[at] = jnp.where(side == 0, one, two).astype(bf16)
                send_ref[at] = jnp.where(side == 0, two, one).astype(bf16)


def backward_kernel(
    slot_rows_ref,
    id_rows_ref,
    cot_ref,
    latent_ref,
    grad_latent_ref,
    down_ref,
    up_ref,
    bias_ref,
    cold_ref,
    hot_ref,
    grads,
):
    fields, samples = slot_rows_ref.shape
    slots, width = cold_ref.shape
    hot_rows = hot_ref.shape[0]
    latent = latent_ref[...]
    grad_latent = grad_latent_ref[...]
    for f in range(fields):
        cols = slice(f * width, (f + 1) * width)
        mixing = (
            jnp.dot(latent, up_ref[:, cols], preferred_element_type=f32) + bias_ref[:, cols]
        )
        back = lax.dot_general(
            grad_latent, down_ref[cols, :], (((1,), (1,)), ((), ())), preferred_element_type=f32
        )
        grad = cot_ref[:, cols].astype(f32) * (mixing + 1.0) + back
        high = grad.astype(bf16)
        rows = slice(f * samples, (f + 1) * samples)
        grads[rows, :width] = high
        grads[rows, width:] = (grad - high.astype(f32)).astype(bf16)
    slot_rows = slot_rows_ref[...]
    id_rows = jnp.where(slot_rows < 0, id_rows_ref[...], -1)
    block = 256
    for rows_of, total, ref, wide in (
        (slot_rows, slots, cold_ref, False),
        (id_rows, hot_rows, hot_ref, True),
    ):
        for first in range(0, total, block):
            place = lax.broadcasted_iota(jnp.int32, (block, samples), 0) + first
            hot = jnp.concatenate(
                [one_hot(rows_of[f : f + 1, :] == place) for f in range(fields)], axis=1
            )
            if wide:
                both = jnp.dot(hot, grads[...], preferred_element_type=f32)
                result = both[:, :width] + both[:, width:]
            else:
                result = jnp.dot(hot, grads[:, :width], preferred_element_type=f32)
            ref[first : first + block, :] = result.astype(bf16)


def cold_adam_kernel(
    scale, req_ref, ret_ref, table_ref, m_ref, v_ref, new_ref, m_new_ref, v_new_ref
):
    lists = req_ref.shape[0]
    block = table_ref.shape[0]
    place = lax.broadcasted_iota(jnp.int32, (block, LANES), 0) + pl.program_id(0) * block
    hot = jnp.concatenate(
        [one_hot(req_ref[i : i + 1, :] == place) for i in range(lists)], axis=1
    )
    total = jnp.dot(hot, ret_ref[...], preferred_element_type=f32) * scale
    new, m_new, v_new = adam_update(table_ref[...], m_ref[...], v_ref[...], total)
    new_ref[...] = new
    m_new_ref[...] = m_new
    v_new_ref[...] = v_new


def cold_adam(req, returned, table, m, v, scale):
    rows, width = table.shape
    block = 256
    tile = pl.BlockSpec((block, width), lambda i: (i, 0))
    whole = lambda a: pl.BlockSpec(a.shape, lambda i: (0, 0))
    like = jax.ShapeDtypeStruct(table.shape, f32)
    return pl.pallas_call(
        functools.partial(cold_adam_kernel, scale),
        grid=(rows // block,),
        in_specs=[whole(req), whole(returned), tile, tile, tile],
        out_specs=[tile] * 3,
        out_shape=[like] * 3,
        compiler_params=pltpu.CompilerParams(vmem_limit_bytes=48 << 20),
        cost_estimate=pl.CostEstimate(
            flops=4 * rows * width * returned.shape[0],
            bytes_accessed=24 * rows * width,
            transcendentals=0,
        ),
        name="cold_adam",
    )(req, returned, table, m, v)


def split_levels(devices):
    cores = 2 if devices % 2 == 0 else 1
    chips = devices // cores
    bits = chips.bit_length() - 1
    if chips != 1 << bits:
        return (chips, 1, 1, cores)
    low = bits // 3
    mid = (bits - low) // 2
    return (1 << (bits - low - mid), 1 << mid, 1 << low, cores)


def body(
    sizes,
    cotangent,
    hot_table,
    cold_table,
    cold_m,
    cold_v,
    cross_down,
    cross_up,
    cross_bias,
    dense_master,
    dense_m,
    dense_v,
    hot_ids,
    lookup_slot,
    fetch_rows,
):
    devices = lax.axis_size("dev")
    sample_count, fields = hot_ids.shape
    slab_rows, emb_width = cold_table.shape
    hot_rows = hot_table.shape[0]
    capacity = fetch_rows.shape[2]
    cross_width, rank = cross_down.shape
    shard = dense_master.shape[0]
    scale_mean = 1.0 / devices
    slots = devices * capacity
    SDS = jax.ShapeDtypeStruct

    me = lax.axis_index("dev")
    strides = [1] * 4
    for i in (2, 1, 0):
        strides[i] = strides[i + 1] * sizes[i + 1]
    digits = [(me // strides[i]) % sizes[i] for i in range(4)]

    def exchange(value, level, k):
        size, stride = sizes[level], strides[level]
        pairs = []
        for d in range(devices):
            digit = (d // stride) % size
            pairs.append((d, d + ((digit + k) % size - digit) * stride))
        return lax.ppermute(value, "dev", pairs)

    def reduce_over(value, level, axis):
        size, digit = sizes[level], digits[level]
        total = lax.dynamic_index_in_dim(value, digit, axis, keepdims=False).astype(f32)
        for k in range(1, size):
            out = lax.dynamic_index_in_dim(value, (digit + k) % size, axis, keepdims=False)
            total = total + exchange(out.astype(bf16), level, k).astype(f32)
        return total

    def reduce_chips(value, order):
        left = [0, 1, 2]
        for level in order:
            value = reduce_over(value, level, left.index(level))
            left.remove(level)
        return value

    def gather_over(value, level, axis):
        size, digit = sizes[level], digits[level]
        parts = [value] + [exchange(value, level, k) for k in range(1, size)]
        if size == 1:
            return jnp.expand_dims(value, axis)
        if size == 2:
            first = jnp.where(digit == 0, parts[0], parts[1])
            second = jnp.where(digit == 0, parts[1], parts[0])
            return jnp.stack([first, second], axis)
        stacked = jnp.stack(parts[::-1] + parts[:0:-1], axis)
        return lax.dynamic_slice_in_dim(stacked, size - 1 - digit, size, axis)

    def gather_chips(value, order):
        have = []
        for level in order:
            have = sorted(have + [level])
            value = gather_over(value, level, have.index(level))
        return value

    requests = lax.all_to_all(fetch_rows, "dev", split_axis=1, concat_axis=0, tiled=True)
    req = requests.reshape(slots // LANES, LANES)
    (picked,) = call(
        owner_pick_kernel,
        [SDS((slots, emb_width), bf16)],
        [req, cold_table],
        4 * slots * slab_rows * emb_width,
        "owner_pick",
        scratch=[pltpu.VMEM((slab_rows, emb_width), bf16)],
    )
    fetched = lax.all_to_all(
        picked.reshape(devices, capacity, emb_width), "dev", split_axis=0, concat_axis=0, tiled=True
    ).reshape(slots, emb_width)
    (hot_x0,) = call(
        hot_pick_kernel,
        [SDS((sample_count, cross_width), bf16)],
        [hot_ids, lookup_slot, hot_table],
        4 * sample_count * fields * hot_rows * emb_width,
        "hot_pick",
    )
    chips = devices // sizes[3]
    part = SDS((chips, shard, rank), bf16)
    latent, grad_latent, bias_part, keep_down, send_down, keep_up, send_up = call(
        forward_kernel,
        [
            SDS((sample_count, rank), bf16),
            SDS((sample_count, rank), bf16),
            SDS((1, cross_width), f32),
            part,
            part,
            part,
            part,
        ],
        [
            digits[3].astype(jnp.int32).reshape(1),
            lookup_slot,
            fetched,
            hot_x0,
            cotangent,
            cross_down,
            cross_up,
        ],
        4 * sample_count * fields * slots * emb_width,
        "forward",
        smem=(0,),
        scratch=[pltpu.VMEM((sample_count, cross_width), bf16)] * 2,
    )
    cold_part, hot_part = call(
        backward_kernel,
        [SDS((slots, emb_width), bf16), SDS((hot_rows, emb_width), bf16)],
        [
            lookup_slot.T,
            hot_ids.T,
            cotangent,
            latent,
            grad_latent,
            cross_down,
            cross_up,
            cross_bias.reshape(1, cross_width),
        ],
        4 * sample_count * fields * (slots + hot_rows) * emb_width,
        "backward",
        scratch=[pltpu.VMEM((sample_count * fields, 2 * emb_width), bf16)],
    )
    returned = lax.all_to_all(
        cold_part.reshape(devices, capacity, emb_width),
        "dev",
        split_axis=0,
        concat_axis=0,
        tiled=True,
    ).reshape(slots, emb_width)

    chip_dims = sizes[:3]

    def chip_sum(keep, send):
        total = keep.astype(f32) + exchange(send, 3, 1).astype(f32)
        return total.reshape(chip_dims + total.shape[1:])

    down_own = reduce_chips(chip_sum(keep_down, send_down), (2, 1, 0))
    up_own = reduce_chips(chip_sum(keep_up, send_up), (1, 2, 0))

    own_hot = hot_rows // devices
    own_bias = cross_width // devices
    extra = 16
    bias_rows = jnp.pad(
        bias_part.reshape(devices, 1, own_bias).astype(bf16),
        ((0, 0), (0, extra - 1), (0, emb_width - own_bias)),
    )
    small = jnp.concatenate(
        [hot_part.reshape(devices, own_hot, emb_width), bias_rows], axis=1
    ).reshape(sizes + (own_hot + extra, emb_width))
    small_own = reduce_chips(reduce_over(small, 3, 3), (1, 2, 0))

    master_new, dense_m_new, dense_v_new = adam_update(
        dense_master,
        dense_m,
        dense_v,
        jnp.concatenate([down_own, up_own], axis=1) * scale_mean,
    )
    weights = master_new.astype(bf16)
    down_all = gather_over(gather_chips(weights[:, :rank], (0, 1, 2)), 3, 3)
    up_all = gather_over(gather_chips(weights[:, rank:], (0, 2, 1)), 3, 3)
    new_weights = jnp.concatenate([down_all, up_all], axis=5).reshape(cross_width, 2 * rank)
    small_all = gather_over(gather_chips((small_own * scale_mean).astype(bf16), (0, 1, 2)), 3, 3)
    small_all = small_all.reshape(devices, own_hot + extra, emb_width).astype(f32)
    hot_grad = small_all[:, :own_hot].reshape(hot_rows, emb_width)
    bias_grad = small_all[:, own_hot, :own_bias].reshape(cross_width)

    cold_new, cold_m_new, cold_v_new = cold_adam(
        req, returned, cold_table, cold_m, cold_v, scale_mean
    )
    return (
        hot_grad,
        bias_grad,
        cold_new,
        cold_m_new,
        cold_v_new,
        master_new,
        dense_m_new,
        dense_v_new,
        new_weights,
    )


def solution(mesh):
    sizes = split_levels(mesh.shape["dev"])
    return jax.shard_map(
        functools.partial(body, sizes),
        mesh=mesh,
        in_specs=(
            P("dev", None),
            P(),
            P("dev", None),
            P("dev", None),
            P("dev", None),
            P(),
            P(),
            P(),
            P("dev", None),
            P("dev", None),
            P("dev", None),
            P("dev", None),
            P("dev", None),
            P("dev", None, None),
        ),
        out_specs=(
            P(),
            P(),
            P("dev", None),
            P("dev", None),
            P("dev", None),
            P("dev", None),
            P("dev", None),
            P("dev", None),
            P(),
        ),
        check_vma=False,
    )
```

```python
import functools

import jax
import jax.numpy as jnp
from jax import lax
from jax.experimental import pallas as pl
from jax.experimental.pallas import tpu as pltpu
from jax.sharding import PartitionSpec as P

first_decay = 0.9
second_decay = 0.999
adam_epsilon = 1e-08
learn_rate = 0.01
first_fix = 1.0 - (0.9**10) ** 10
second_fix = 1.0 - (0.999**10) ** 10

LANES = 128
VMEM_MOST = 48 << 20
f32 = jnp.float32
bf16 = jnp.bfloat16


def adam_update(params, moment_one, moment_two, gradient):
    moment_one = first_decay * moment_one + (1.0 - first_decay) * gradient
    moment_two = second_decay * moment_two + (1.0 - second_decay) * gradient * gradient
    params = params - learn_rate * (moment_one / first_fix) / (
        jnp.sqrt(moment_two / second_fix) + adam_epsilon
    )
    return (params, moment_one, moment_two)


def call(kernel, outs, args, flops, name, smem=(), hbm=(), out_hbm=(), scratch=(), vmem=24 << 20):
    specs = [
        pl.BlockSpec(
            memory_space=pltpu.SMEM if i in smem else pl.ANY if i in hbm else pltpu.VMEM
        )
        for i in range(len(args))
    ]
    moved = sum(a.size * a.dtype.itemsize for a in list(args) + list(outs))
    return pl.pallas_call(
        kernel,
        out_shape=outs,
        in_specs=specs,
        out_specs=[
            pl.BlockSpec(memory_space=pl.ANY if i in out_hbm else pltpu.VMEM)
            for i in range(len(outs))
        ],
        scratch_shapes=list(scratch),
        compiler_params=pltpu.CompilerParams(vmem_limit_bytes=vmem),
        cost_estimate=pl.CostEstimate(flops=flops, bytes_accessed=moved, transcendentals=0),
        name=name,
    )(*args)


def one_hot(mask):
    return jnp.where(mask, 1.0, 0.0).astype(bf16)


def ways(rows):
    return 4 if rows % 64 == 0 else 1


def fold(index, rows):
    part = rows // ways(rows)
    block = jnp.zeros_like(index)
    for j in range(1, ways(rows)):
        block = block + jnp.where(index >= j * part, 1, 0)
    return block, index - block * part


def lay_beside(table, out_ref):
    rows, width = table.shape
    part = rows // ways(rows)
    for j in range(ways(rows)):
        out_ref[:, j * width : (j + 1) * width] = table[j * part : (j + 1) * part].astype(bf16)


def pick_rows(block, place, folded, width):
    part = folded.shape[0]
    hot = one_hot(place == lax.broadcasted_iota(jnp.int32, (place.shape[0], part), 1))
    both = jnp.dot(hot, folded[...], preferred_element_type=f32)
    out = both[:, :width]
    for j in range(1, both.shape[1] // width):
        out = jnp.where(block == j, both[:, j * width : (j + 1) * width], out)
    return out


def columns_of(lists):
    turned = jnp.transpose(lists)
    return jnp.concatenate([turned[:, i : i + 1] for i in range(lists.shape[0])], axis=0)


def fold_table_kernel(table_ref, out_ref):
    lay_beside(table_ref[...], out_ref)


def fold_table(table):
    rows, width = table.shape
    return call(
        fold_table_kernel,
        [jax.ShapeDtypeStruct((rows // ways(rows), ways(rows) * width), bf16)],
        [table],
        0,
        "fold_table",
    )[0]


def owner_pick_kernel(rows, req_ref, folded_ref, out_ref):
    slots, width = out_ref.shape
    column = columns_of(req_ref[:, 0, :])
    block, place = fold(column, rows)
    step = 512 if slots % 512 == 0 else slots
    for first in range(0, slots, step):
        at = slice(first, first + step)
        out_ref[at, :] = pick_rows(block[at], place[at], folded_ref, width).astype(bf16)


def hot_pick_kernel(ids_ref, slot_ref, table_ref, out_ref, folded):
    samples, fields = ids_ref.shape
    rows, width = table_ref.shape
    lay_beside(table_ref[...], folded)
    block, place = fold(jnp.where(slot_ref[...] < 0, ids_ref[...], -1), rows)
    for f in range(fields):
        out_ref[:, f * width : (f + 1) * width] = pick_rows(
            block[:, f : f + 1], place[:, f : f + 1], folded, width
        ).astype(bf16)


def store_halves(digits_ref, dims, order, sums, first, keep_ref, send_ref):
    shard = keep_ref.shape[-2]
    side = digits_ref[3]
    for j in range(sums.shape[0] // (2 * shard)):
        one = sums[2 * j * shard : (2 * j + 1) * shard]
        two = sums[(2 * j + 1) * shard : (2 * j + 2) * shard]
        chip = first // (2 * shard) + j
        digit = (chip // (dims[1] * dims[2]), chip // dims[2] % dims[1], chip % dims[2])
        at = tuple(
            lax.rem(digit[level] - digits_ref[level] + dims[level], dims[level])
            for level in order
        )
        keep_ref[at] = jnp.where(side == 0, one, two).astype(bf16)
        send_ref[at] = jnp.where(side == 0, two, one).astype(bf16)


def outer_sums(digits_ref, dims, order, left, right, keep_ref, send_ref):
    block = max(2 * keep_ref.shape[-2], 256)
    for first in range(0, left.shape[1], block):
        sums = lax.dot_general(
            left[:, first : first + block],
            right,
            (((0,), (0,)), ((), ())),
            preferred_element_type=f32,
        )
        store_halves(digits_ref, dims, order, sums, first, keep_ref, send_ref)


def start_copies(sems, pairs, first=0):
    copies = [
        pltpu.make_async_copy(source, target, sems.at[first + i])
        for i, (source, target) in enumerate(pairs)
    ]
    for copy in copies:
        copy.start()
    return copies


def forward_kernel(
    dims,
    order_a,
    order_b,
    digits_ref,
    slot_ref,
    fetched_ref,
    cross_bias_ref,
    hot_hbm,
    cot_hbm,
    down_hbm,
    up_hbm,
    bias_ref,
    keep_a_hbm,
    send_a_hbm,
    keep_b_hbm,
    send_b_hbm,
    grad_hbm,
    x0,
    gm,
    folded,
    hot_ref,
    cot_ref,
    down_ref,
    up_ref,
    keep_a,
    send_a,
    keep_b,
    send_b,
    grad_ref,
    sems,
):
    copies = start_copies(
        sems, ((hot_hbm, hot_ref), (cot_hbm, cot_ref), (up_hbm, up_ref), (down_hbm, down_ref))
    )
    samples, fields = slot_ref.shape
    slots, width = fetched_ref.shape
    lay_beside(fetched_ref[...], folded)
    block, place = fold(slot_ref[...], slots)
    for f in range(fields):
        cols = slice(f * width, (f + 1) * width)
        cold = pick_rows(block[:, f : f + 1], place[:, f : f + 1], folded, width)
        if f == 0:
            copies[0].wait()
            copies[1].wait()
        picked = cold + hot_ref[:, cols].astype(f32)
        x0[:, cols] = picked.astype(bf16)
        mix = (cot_ref[:, cols].astype(f32) * picked).astype(bf16)
        gm[:, cols] = mix
        bias_ref[f : f + 1, :] = jnp.sum(mix.astype(f32), axis=0, keepdims=True)
    copies[2].wait()
    grad_latent = lax.dot_general(
        gm[...], up_ref[...], (((1,), (1,)), ((), ())), preferred_element_type=f32
    ).astype(bf16)
    outer_sums(digits_ref, dims, order_a, x0, grad_latent, keep_a, send_a)
    done = start_copies(sems, ((send_a, send_a_hbm), (keep_a, keep_a_hbm)), 4)
    copies[3].wait()
    latent = jnp.dot(x0[...], down_ref[...], preferred_element_type=f32).astype(bf16)
    outer_sums(digits_ref, dims, order_b, gm, latent, keep_b, send_b)
    done += start_copies(sems, ((send_b, send_b_hbm), (keep_b, keep_b_hbm)), 6)
    step = 4 if fields % 4 == 0 else fields
    for f in range(fields):
        cols = slice(f * width, (f + 1) * width)
        mixing = (
            jnp.dot(latent, up_ref[:, cols], preferred_element_type=f32) + cross_bias_ref[:, cols]
        )
        back = lax.dot_general(
            grad_latent, down_ref[cols, :], (((1,), (1,)), ((), ())), preferred_element_type=f32
        )
        grad = cot_ref[:, cols].astype(f32) * (mixing + 1.0) + back
        grad_ref[:, cols] = grad.astype(bf16)
        if (f + 1) % step == 0:
            part = slice((f + 1 - step) * width, (f + 1) * width)
            done += start_copies(
                sems, ((grad_ref.at[:, part], grad_hbm.at[:, part]),), 8 + f // step
            )
    for copy in done:
        copy.wait()


def add_up(lists, total, grads, use):
    fields, samples = lists.shape
    unused, place = fold(lists, total)
    part = total // ways(total)
    width = grads.shape[1] // ways(total)
    step = 256 if part % 256 == 0 else part
    for first in range(0, part, step):
        spot = lax.broadcasted_iota(jnp.int32, (step, samples), 0) + first
        hot = jnp.concatenate(
            [one_hot(place[f : f + 1, :] == spot) for f in range(fields)], axis=1
        )
        sums = jnp.dot(hot, grads[...], preferred_element_type=f32)
        for j in range(ways(total)):
            use(j * part + first, sums[:, j * width : (j + 1) * width])


def lay_by_block(block, grad, grads, rows):
    width = grad.shape[1]
    for j in range(grads.shape[1] // width):
        grads[rows, j * width : (j + 1) * width] = jnp.where(block == j, grad, 0.0).astype(bf16)


def lay_all_by_block(index, total, grad_ref, grads):
    samples, fields = index.shape
    width = grad_ref.shape[1] // fields
    block, unused = fold(index, total)
    for f in range(fields):
        lay_by_block(
            block[:, f : f + 1],
            grad_ref[:, f * width : (f + 1) * width].astype(f32),
            grads,
            slice(f * samples, (f + 1) * samples),
        )


def hot_sums_kernel(dims, order, digits_ref, id_ref, id_rows_ref, grad_ref, keep_ref, send_ref, grads):
    hot_rows = 2 * keep_ref.size // keep_ref.shape[-1]
    lay_all_by_block(id_ref[...], hot_rows, grad_ref, grads)

    def use(first, sums):
        store_halves(digits_ref, dims, order, sums, first, keep_ref, send_ref)

    add_up(id_rows_ref[...], hot_rows, grads, use)


def cold_sums_kernel(slot_ref, slot_rows_ref, grad_ref, bias_ref, cold_ref, grads):
    fields = slot_ref.shape[1]
    devices, capacity, width = cold_ref.shape
    capacity -= fields
    slots = devices * capacity
    lay_all_by_block(slot_ref[...], slots, grad_ref, grads)

    def use(first, sums):
        sums = sums.astype(bf16)
        at, end = first, first + sums.shape[0]
        while at < end:
            owner, slot = at // capacity, at % capacity
            count = min(capacity - slot, end - at)
            cold_ref[owner, slot : slot + count, :] = sums[at - first : at - first + count]
            at += count

    add_up(slot_rows_ref[...], slots, grads, use)
    bias = bias_ref[...].astype(bf16)
    for owner in range(devices):
        cold_ref[owner, capacity:, :] = bias


def cold_adam_kernel(
    scale, req_ref, ret_ref, table_ref, m_ref, v_ref, new_ref, m_new_ref, v_new_ref, spread
):
    lists = req_ref.shape[0]
    rows, width = table_ref.shape
    req = req_ref[...]
    block, unused = fold(columns_of(req), rows)
    returned = ret_ref[...].astype(f32)
    for j in range(ways(rows)):
        spread[:, j * width : (j + 1) * width] = jnp.where(block == j, returned, 0.0).astype(bf16)
    unused, place = fold(req, rows)
    part = rows // ways(rows)
    step = 256 if part % 256 == 0 else part
    for first in range(0, part, step):
        spot = lax.broadcasted_iota(jnp.int32, (step, LANES), 0) + first
        hot = jnp.concatenate(
            [one_hot(place[i : i + 1, :] == spot) for i in range(lists)], axis=1
        )
        sums = jnp.dot(hot, spread[...], preferred_element_type=f32)
        for j in range(ways(rows)):
            at = slice(j * part + first, j * part + first + step)
            new_ref[at, :], m_new_ref[at, :], v_new_ref[at, :] = adam_update(
                table_ref[at, :],
                m_ref[at, :],
                v_ref[at, :],
                sums[:, j * width : (j + 1) * width] * scale,
            )


def place_kernel(dims, plan, digits_ref, *refs):
    sources = refs[: len(plan)]
    out, hot_out, hot_rows, sems = refs[-4:]
    shard = sources[0].shape[-2]
    half = out.shape[1] // 2
    copies = []
    hots = 0
    for ref, (cols, main, k, core) in zip(sources, plan):
        other = 3 - main
        for i in range(ref.shape[0]):
            for j in range(ref.shape[1]):
                turn = {0: j, main: k, other: i}
                digit = [
                    lax.rem(digits_ref[level] - turn[level] + dims[level], dims[level])
                    for level in range(3)
                ]
                chip = (digit[0] * dims[1] + digit[1]) * dims[2] + digit[2]
                side = lax.rem(digits_ref[3] + core, 2)
                row = pl.multiple_of((chip * 2 + side) * shard, shard)
                copies.append(
                    (ref.at[i, j, :, :half], out.at[pl.ds(row, shard), pl.ds(cols * half, half)])
                )
                if cols == 0:
                    hot_rows[hots] = ref[i, j, :, half:].astype(f32)
                    copies.append((hot_rows.at[hots], hot_out.at[pl.ds(row, shard), :]))
                    hots += 1
    for copy in start_copies(sems, copies):
        copy.wait()


def place(dims, plan, digits, sources, rank, devices, before):
    shard, split = sources[0].shape[-2:]
    rows = shard * devices
    before = list(before or ())
    hbm, vmem = pl.BlockSpec(memory_space=pl.ANY), pl.BlockSpec(memory_space=pltpu.VMEM)
    first = 1 + len(sources)
    blocks = [s.shape[0] * s.shape[1] for s in sources]
    hots = sum(b for b, p in zip(blocks, plan) if p[0] == 0)
    return pl.pallas_call(
        functools.partial(place_kernel, dims, tuple(plan)),
        out_shape=[
            jax.ShapeDtypeStruct((rows, 2 * rank), bf16),
            jax.ShapeDtypeStruct((rows, split - rank), f32),
        ],
        in_specs=[pl.BlockSpec(memory_space=pltpu.SMEM)]
        + [vmem] * len(sources)
        + [hbm] * len(before),
        out_specs=[hbm, hbm],
        input_output_aliases={first + i: i for i in range(len(before))},
        scratch_shapes=[
            pltpu.VMEM((hots, shard, split - rank), f32),
            pltpu.SemaphoreType.DMA((sum(blocks) + hots,)),
        ],
        compiler_params=pltpu.CompilerParams(vmem_limit_bytes=24 << 20),
        cost_estimate=pl.CostEstimate(
            flops=0, bytes_accessed=4 * rows * rank, transcendentals=0
        ),
        name="place",
    )(digits, *sources, *before)


def split_levels(devices):
    cores = 2 if devices % 2 == 0 else 1
    chips = devices // cores
    bits = chips.bit_length() - 1
    if chips != 1 << bits:
        return (chips, 1, 1, cores)
    low = bits // 3
    mid = (bits - low) // 2
    return (1 << (bits - low - mid), 1 << mid, 1 << low, cores)


def body(
    sizes,
    cotangent,
    hot_table,
    cold_table,
    cold_m,
    cold_v,
    cross_down,
    cross_up,
    cross_bias,
    dense_master,
    dense_m,
    dense_v,
    hot_ids,
    lookup_slot,
    fetch_rows,
):
    devices = lax.axis_size("dev")
    sample_count, fields = hot_ids.shape
    slab_rows, emb_width = cold_table.shape
    hot_rows = hot_table.shape[0]
    capacity = fetch_rows.shape[2]
    cross_width, rank = cross_down.shape
    shard = dense_master.shape[0]
    scale_mean = 1.0 / devices
    slots = devices * capacity
    lookups = sample_count * fields
    dims = sizes[:3]
    SDS = jax.ShapeDtypeStruct

    me = lax.axis_index("dev")
    strides = [1] * 4
    for i in (2, 1, 0):
        strides[i] = strides[i + 1] * sizes[i + 1]
    digits = jnp.stack([(me // strides[i]) % sizes[i] for i in range(4)]).astype(jnp.int32)

    def exchange(value, level, k):
        size, stride = sizes[level], strides[level]
        pairs = []
        for d in range(devices):
            digit = (d // stride) % size
            pairs.append((d, d + ((digit + k) % size - digit) * stride))
        return lax.ppermute(value, "dev", pairs)

    def swap(value):
        return exchange(value, 3, 1) if sizes[3] == 2 else None

    def all_to_all(value):
        return lax.all_to_all(value, "dev", split_axis=0, concat_axis=0, tiled=True)

    folded = fold_table(cold_table)
    (hot_x0,) = call(
        hot_pick_kernel,
        [SDS((sample_count, cross_width), bf16)],
        [hot_ids, lookup_slot, hot_table],
        40 * lookups * hot_rows * emb_width,
        "hot_pick",
        scratch=[pltpu.VMEM((hot_rows // ways(hot_rows), ways(hot_rows) * emb_width), bf16)],
    )
    requests = all_to_all(fetch_rows.reshape(devices, 1, capacity))
    req = requests.reshape(slots // LANES, LANES)
    (picked,) = call(
        functools.partial(owner_pick_kernel, slab_rows),
        [SDS((slots, emb_width), bf16)],
        [requests, folded],
        4 * slots * slab_rows * emb_width,
        "owner_pick",
    )
    fetched = all_to_all(picked.reshape(devices, capacity, emb_width)).reshape(slots, emb_width)

    order_a, order_b = (2, 1, 0), (1, 2, 0)
    shape_a = tuple(dims[i] for i in order_a) + (shard, rank)
    shape_b = tuple(dims[i] for i in order_b) + (shard, rank)
    bias_part, keep_a, send_a, keep_b, send_b, grad_input = call(
        functools.partial(forward_kernel, dims, order_a, order_b),
        [
            SDS((fields, emb_width), f32),
            SDS(shape_a, bf16),
            SDS(shape_a, bf16),
            SDS(shape_b, bf16),
            SDS(shape_b, bf16),
            SDS((sample_count, cross_width), bf16),
        ],
        [
            digits,
            lookup_slot,
            fetched,
            cross_bias.reshape(1, cross_width),
            hot_x0,
            cotangent,
            cross_down,
            cross_up,
        ],
        4 * lookups * slots * emb_width,
        "forward",
        smem=(0,),
        hbm=(4, 5, 6, 7),
        out_hbm=(1, 2, 3, 4, 5),
        scratch=[
            pltpu.VMEM((sample_count, cross_width), bf16),
            pltpu.VMEM((sample_count, cross_width), bf16),
            pltpu.VMEM((slots // ways(slots), ways(slots) * emb_width), bf16),
            pltpu.VMEM((sample_count, cross_width), bf16),
            pltpu.VMEM((sample_count, cross_width), bf16),
            pltpu.VMEM(cross_down.shape, bf16),
            pltpu.VMEM(cross_up.shape, bf16),
            pltpu.VMEM(shape_a, bf16),
            pltpu.VMEM(shape_a, bf16),
            pltpu.VMEM(shape_b, bf16),
            pltpu.VMEM(shape_b, bf16),
            pltpu.VMEM((sample_count, cross_width), bf16),
            pltpu.SemaphoreType.DMA((8 + fields,)),
        ],
        vmem=VMEM_MOST,
    )
    got_a = swap(send_a)
    got_b = swap(send_b)
    own_hot = hot_rows // devices
    shape_hot = tuple(dims[i] for i in order_a) + (own_hot, emb_width)
    hot_index = jnp.where(lookup_slot < 0, hot_ids, -1)
    keep_hot, send_hot = call(
        functools.partial(hot_sums_kernel, dims, order_a),
        [SDS(shape_hot, bf16), SDS(shape_hot, bf16)],
        [digits, hot_index, hot_index.T, grad_input],
        4 * lookups * hot_rows * emb_width,
        "hot_sums",
        smem=(0,),
        scratch=[pltpu.VMEM((lookups, ways(hot_rows) * emb_width), bf16)],
        vmem=VMEM_MOST,
    )
    got_hot = swap(send_hot)

    def add(terms, *at):
        return functools.reduce(
            lambda s, t: s + t, [t[skip + at].astype(f32) for t, skip in terms]
        )

    def pack(groups, *at):
        return jnp.concatenate([add(terms, *at) for terms in groups], axis=-1)

    def step_sends(groups, level):
        return [pack(groups, k).astype(bf16) for k in range(1, sizes[level])]

    def step_takes(groups, level, sends):
        later = [[(t, skip + (0,)) for t, skip in terms] for terms in groups]
        for k, send in enumerate(sends):
            got = exchange(send, level, k + 1)
            start = 0
            for terms, old in zip(later, groups):
                wide = old[0][0].shape[-1]
                terms.append((got[..., start : start + wide], ()))
                start += wide
        return later

    groups_b = [[(keep_b, ()), (got_b, ())]]
    groups_a = [[(keep_a, ()), (got_a, ())], [(keep_hot, ()), (got_hot, ())]]
    sends_b = step_sends(groups_b, order_b[0])
    sends_a = step_sends(groups_a, order_a[0])
    grad_input, sends_a, sends_b = lax.optimization_barrier((grad_input, sends_a, sends_b))
    groups_b = step_takes(groups_b, order_b[0], sends_b)
    groups_a = step_takes(groups_a, order_a[0], sends_a)
    whole = capacity % 16 == 0
    (parcel,) = call(
        cold_sums_kernel,
        [
            SDS(
                (devices, capacity + fields, emb_width) if whole else (1, slots + fields, emb_width),
                bf16,
            )
        ],
        [lookup_slot, lookup_slot.T, grad_input, bias_part],
        4 * lookups * slots * emb_width,
        "cold_sums",
        scratch=[pltpu.VMEM((lookups, ways(slots) * emb_width), bf16)],
        vmem=VMEM_MOST,
    )
    if not whole:
        parcel = jnp.concatenate(
            [
                parcel[0, :slots].reshape(devices, capacity, emb_width),
                jnp.broadcast_to(parcel[:, slots:], (devices, fields, emb_width)),
            ],
            axis=1,
        )
    arrived = all_to_all(parcel)
    groups_b = step_takes(groups_b, order_b[1], step_sends(groups_b, order_b[1]))
    groups_a = step_takes(groups_a, order_a[1], step_sends(groups_a, order_a[1]))
    groups = [groups_a[0], groups_b[0], groups_a[1]]
    sums = [pack(groups, k) for k in range(sizes[0])]

    returned = arrived[:, :capacity].reshape(slots, emb_width)
    like = SDS(cold_table.shape, f32)
    cold_new, cold_m_new, cold_v_new = call(
        functools.partial(cold_adam_kernel, scale_mean),
        [like] * 3,
        [req, returned, cold_table, cold_m, cold_v],
        4 * slots * slab_rows * emb_width,
        "cold_adam",
        scratch=[pltpu.VMEM((slots, ways(slab_rows) * emb_width), bf16)],
    )
    bias_grad = (
        jnp.sum(arrived[:, capacity:].astype(f32), axis=0) * scale_mean
    ).reshape(cross_width)

    later = [exchange(sums[k].astype(bf16), 0, k) for k in range(1, sizes[0])]
    later, cold_new, cold_m_new, cold_v_new, bias_grad = lax.optimization_barrier(
        (later, cold_new, cold_m_new, cold_v_new, bias_grad)
    )
    dense_own = sums[0]
    for got in later:
        dense_own = dense_own + got.astype(f32)

    master_new, dense_m_new, dense_v_new = adam_update(
        dense_master, dense_m, dense_v, dense_own[:, : 2 * rank] * scale_mean
    )
    weights = jnp.concatenate(
        [master_new[:, :rank], dense_own[:, 2 * rank :] * scale_mean, master_new[:, rank:]], axis=1
    ).astype(bf16)
    split = rank + emb_width
    along_z = [weights] + [exchange(weights, 0, k) for k in range(1, sizes[0])]
    plan, got = [], []
    for cols, (level, main) in enumerate(((1, 2), (2, 1))):
        block = jnp.stack([w[:, split:] if cols else w[:, :split] for w in along_z])
        block = jnp.stack(
            [block] + [exchange(block, level, k) for k in range(1, sizes[level])]
        )
        for k in range(sizes[main]):
            plan.append((cols, main, k))
            got.append(exchange(block, main, k) if k else block)

    def put(which, core, values, before):
        return place(
            dims, [plan[i] + (core,) for i in which], digits, values, rank, devices, before
        )

    near = [i for i, p in enumerate(plan) if p[2] == 0]
    far = [i for i, p in enumerate(plan) if p[2] > 0]
    outs = put(near, 0, [got[i] for i in near], None)
    outs = put(near, 1, [swap(got[i]) for i in near], outs)
    if far:
        values, outs = lax.optimization_barrier(([got[i] for i in far], outs))
        others = [swap(v) for v in values]
        outs = put(far, 0, values, outs)
        outs = put(far, 1, others, outs)
    new_weights, hot_grad = outs
    return (
        hot_grad,
        bias_grad,
        cold_new,
        cold_m_new,
        cold_v_new,
        master_new,
        dense_m_new,
        dense_v_new,
        new_weights,
    )


def solution(mesh):
    sizes = split_levels(mesh.shape["dev"])
    return jax.shard_map(
        functools.partial(body, sizes),
        mesh=mesh,
        in_specs=(
            P("dev", None),
            P(),
            P("dev", None),
            P("dev", None),
            P("dev", None),
            P(),
            P(),
            P(),
            P("dev", None),
            P("dev", None),
            P("dev", None),
            P("dev", None),
            P("dev", None),
            P("dev", None, None),
        ),
        out_specs=(
            P(),
            P(),
            P("dev", None),
            P("dev", None),
            P("dev", None),
            P("dev", None),
            P("dev", None),
            P("dev", None),
            P(),
        ),
        check_vma=False,
    )
```

```python
import functools

import jax
import jax.numpy as jnp
from jax import lax
from jax.experimental import pallas as pl
from jax.experimental.pallas import tpu as pltpu
from jax.sharding import PartitionSpec as P

first_decay = 0.9
second_decay = 0.999
adam_epsilon = 1e-08
learn_rate = 0.01
first_fix = 1.0 - (0.9**10) ** 10
second_fix = 1.0 - (0.999**10) ** 10

LANES = 128
VMEM_MOST = 48 << 20
f32 = jnp.float32
bf16 = jnp.bfloat16


def adam_update(params, moment_one, moment_two, gradient):
    moment_one = first_decay * moment_one + (1.0 - first_decay) * gradient
    moment_two = second_decay * moment_two + (1.0 - second_decay) * gradient * gradient
    params = params - learn_rate * (moment_one / first_fix) / (
        jnp.sqrt(moment_two / second_fix) + adam_epsilon
    )
    return (params, moment_one, moment_two)


def call(kernel, outs, args, flops, name, smem=(), hbm=(), out_hbm=(), scratch=(), vmem=24 << 20):
    specs = [
        pl.BlockSpec(
            memory_space=pltpu.SMEM if i in smem else pl.ANY if i in hbm else pltpu.VMEM
        )
        for i in range(len(args))
    ]
    moved = sum(a.size * a.dtype.itemsize for a in list(args) + list(outs))
    return pl.pallas_call(
        kernel,
        out_shape=outs,
        in_specs=specs,
        out_specs=[
            pl.BlockSpec(memory_space=pl.ANY if i in out_hbm else pltpu.VMEM)
            for i in range(len(outs))
        ],
        scratch_shapes=list(scratch),
        compiler_params=pltpu.CompilerParams(vmem_limit_bytes=vmem),
        cost_estimate=pl.CostEstimate(flops=flops, bytes_accessed=moved, transcendentals=0),
        name=name,
    )(*args)


def one_hot(mask):
    return jnp.where(mask, 1.0, 0.0).astype(bf16)


def ways(rows):
    return 4 if rows % 64 == 0 else 1


def fold(index, rows):
    part = rows // ways(rows)
    block = jnp.zeros_like(index)
    for j in range(1, ways(rows)):
        block = block + jnp.where(index >= j * part, 1, 0)
    return block, index - block * part


def lay_beside(table, out_ref):
    rows, width = table.shape
    part = rows // ways(rows)
    for j in range(ways(rows)):
        out_ref[:, j * width : (j + 1) * width] = table[j * part : (j + 1) * part].astype(bf16)


def pick_rows(block, place, folded, width):
    part = folded.shape[0]
    hot = one_hot(place == lax.broadcasted_iota(jnp.int32, (place.shape[0], part), 1))
    both = jnp.dot(hot, folded[...], preferred_element_type=f32)
    out = both[:, :width]
    for j in range(1, both.shape[1] // width):
        out = jnp.where(block == j, both[:, j * width : (j + 1) * width], out)
    return out


def stacked(columns, first, count):
    return jnp.concatenate([columns[:, f : f + 1] for f in range(first, first + count)], axis=0)


def columns_of(lists):
    turned = jnp.transpose(lists)
    return jnp.concatenate([turned[:, i : i + 1] for i in range(lists.shape[0])], axis=0)


def fold_table_kernel(table_ref, out_ref):
    lay_beside(table_ref[...], out_ref)


def fold_table(table):
    rows, width = table.shape
    return call(
        fold_table_kernel,
        [jax.ShapeDtypeStruct((rows // ways(rows), ways(rows) * width), bf16)],
        [table],
        0,
        "fold_table",
    )[0]


def owner_pick_kernel(rows, req_ref, folded_ref, out_ref):
    slots, width = out_ref.shape
    column = columns_of(req_ref[:, 0, :])
    block, place = fold(column, rows)
    step = 1024 if slots % 1024 == 0 else slots
    for first in range(0, slots, step):
        at = slice(first, first + step)
        out_ref[at, :] = pick_rows(block[at], place[at], folded_ref, width).astype(bf16)


def hot_pick_kernel(ids_ref, slot_ref, table_ref, out_ref, folded):
    samples, fields = ids_ref.shape
    rows, width = table_ref.shape
    lay_beside(table_ref[...], folded)
    block, place = fold(jnp.where(slot_ref[...] < 0, ids_ref[...], -1), rows)
    for f in range(fields):
        out_ref[:, f * width : (f + 1) * width] = pick_rows(
            block[:, f : f + 1], place[:, f : f + 1], folded, width
        ).astype(bf16)


def store_halves(digits_ref, dims, order, sums, first, keep_ref, send_ref):
    shard = keep_ref.shape[-2]
    side = digits_ref[3]
    for j in range(sums.shape[0] // (2 * shard)):
        one = sums[2 * j * shard : (2 * j + 1) * shard]
        two = sums[(2 * j + 1) * shard : (2 * j + 2) * shard]
        chip = first // (2 * shard) + j
        digit = (chip // (dims[1] * dims[2]), chip // dims[2] % dims[1], chip % dims[2])
        at = tuple(
            lax.rem(digit[level] - digits_ref[level] + dims[level], dims[level])
            for level in order
        )
        keep_ref[at] = jnp.where(side == 0, one, two).astype(bf16)
        send_ref[at] = jnp.where(side == 0, two, one).astype(bf16)


def outer_sums(digits_ref, dims, order, left, right, keep_ref, send_ref):
    block = max(2 * keep_ref.shape[-2], min(left.shape[1], 1024))
    for first in range(0, left.shape[1], block):
        sums = lax.dot_general(
            left[:, first : first + block],
            right,
            (((0,), (0,)), ((), ())),
            preferred_element_type=f32,
        )
        store_halves(digits_ref, dims, order, sums, first, keep_ref, send_ref)


def start_copies(sems, pairs, first=0):
    copies = [
        pltpu.make_async_copy(source, target, sems.at[first + i])
        for i, (source, target) in enumerate(pairs)
    ]
    for copy in copies:
        copy.start()
    return copies


def forward_kernel(
    dims,
    order_a,
    order_b,
    digits_ref,
    slot_ref,
    fetched_ref,
    cross_bias_ref,
    hot_hbm,
    cot_hbm,
    down_hbm,
    up_hbm,
    bias_ref,
    keep_a_hbm,
    send_a_hbm,
    keep_b_hbm,
    send_b_hbm,
    grad_hbm,
    x0,
    gm,
    folded,
    hot_ref,
    cot_ref,
    down_ref,
    up_ref,
    keep_a,
    send_a,
    keep_b,
    send_b,
    grad_ref,
    sems,
):
    copies = start_copies(
        sems, ((hot_hbm, hot_ref), (cot_hbm, cot_ref), (up_hbm, up_ref), (down_hbm, down_ref))
    )
    samples, fields = slot_ref.shape
    slots, width = fetched_ref.shape
    lay_beside(fetched_ref[...], folded)
    block, place = fold(slot_ref[...], slots)
    group = 4 if fields % 4 == 0 else 1
    for first in range(0, fields, group):
        cold = pick_rows(
            stacked(block, first, group), stacked(place, first, group), folded, width
        )
        if first == 0:
            copies[0].wait()
            copies[1].wait()
        for i in range(group):
            f = first + i
            cols = slice(f * width, (f + 1) * width)
            picked = cold[i * samples : (i + 1) * samples] + hot_ref[:, cols].astype(f32)
            x0[:, cols] = picked.astype(bf16)
            mix = (cot_ref[:, cols].astype(f32) * picked).astype(bf16)
            gm[:, cols] = mix
            bias_ref[f : f + 1, :] = jnp.sum(mix.astype(f32), axis=0, keepdims=True)
    copies[2].wait()
    grad_latent = lax.dot_general(
        gm[...], up_ref[...], (((1,), (1,)), ((), ())), preferred_element_type=f32
    ).astype(bf16)
    outer_sums(digits_ref, dims, order_a, x0, grad_latent, keep_a, send_a)
    done = start_copies(sems, ((send_a, send_a_hbm), (keep_a, keep_a_hbm)), 4)
    copies[3].wait()
    latent = jnp.dot(x0[...], down_ref[...], preferred_element_type=f32).astype(bf16)
    outer_sums(digits_ref, dims, order_b, gm, latent, keep_b, send_b)
    done += start_copies(sems, ((send_b, send_b_hbm), (keep_b, keep_b_hbm)), 6)
    for first in range(0, fields, group):
        cols = slice(first * width, (first + group) * width)
        mixing = (
            jnp.dot(latent, up_ref[:, cols], preferred_element_type=f32) + cross_bias_ref[:, cols]
        )
        back = lax.dot_general(
            grad_latent, down_ref[cols, :], (((1,), (1,)), ((), ())), preferred_element_type=f32
        )
        grad = cot_ref[:, cols].astype(f32) * (mixing + 1.0) + back
        grad_ref[:, cols] = grad.astype(bf16)
        done += start_copies(
            sems, ((grad_ref.at[:, cols], grad_hbm.at[:, cols]),), 8 + first // group
        )
    for copy in done:
        copy.wait()


def add_up(lists, total, grads, use):
    fields, samples = lists.shape
    unused, place = fold(lists, total)
    part = total // ways(total)
    width = grads.shape[1] // ways(total)
    step = part
    for first in range(0, part, step):
        spot = lax.broadcasted_iota(jnp.int32, (step, samples), 0) + first
        hot = jnp.concatenate(
            [one_hot(place[f : f + 1, :] == spot) for f in range(fields)], axis=1
        )
        sums = jnp.dot(hot, grads[...], preferred_element_type=f32)
        for j in range(ways(total)):
            use(j * part + first, sums[:, j * width : (j + 1) * width])


def lay_by_block(block, grad, grads, rows):
    width = grad.shape[1]
    for j in range(grads.shape[1] // width):
        grads[rows, j * width : (j + 1) * width] = jnp.where(block == j, grad, 0.0).astype(bf16)


def lay_all_by_block(index, total, grad_ref, grads):
    samples, fields = index.shape
    width = grad_ref.shape[1] // fields
    block, unused = fold(index, total)
    for f in range(fields):
        lay_by_block(
            block[:, f : f + 1],
            grad_ref[:, f * width : (f + 1) * width].astype(f32),
            grads,
            slice(f * samples, (f + 1) * samples),
        )


def hot_sums_kernel(dims, order, digits_ref, id_ref, id_rows_ref, grad_ref, keep_ref, send_ref, grads):
    hot_rows = 2 * keep_ref.size // keep_ref.shape[-1]
    lay_all_by_block(id_ref[...], hot_rows, grad_ref, grads)

    def use(first, sums):
        store_halves(digits_ref, dims, order, sums, first, keep_ref, send_ref)

    add_up(id_rows_ref[...], hot_rows, grads, use)


def cold_sums_kernel(slot_ref, slot_rows_ref, grad_ref, bias_ref, cold_ref, grads):
    fields = slot_ref.shape[1]
    devices, capacity, width = cold_ref.shape
    capacity -= fields
    slots = devices * capacity
    lay_all_by_block(slot_ref[...], slots, grad_ref, grads)

    def use(first, sums):
        sums = sums.astype(bf16)
        at, end = first, first + sums.shape[0]
        while at < end:
            owner, slot = at // capacity, at % capacity
            count = min(capacity - slot, end - at)
            cold_ref[owner, slot : slot + count, :] = sums[at - first : at - first + count]
            at += count

    add_up(slot_rows_ref[...], slots, grads, use)
    bias = bias_ref[...].astype(bf16)
    for owner in range(devices):
        cold_ref[owner, capacity:, :] = bias


def cold_adam_kernel(
    scale, req_ref, ret_ref, table_ref, m_ref, v_ref, new_ref, m_new_ref, v_new_ref, spread
):
    lists = req_ref.shape[0]
    rows, width = table_ref.shape
    req = req_ref[...]
    block, unused = fold(columns_of(req), rows)
    returned = ret_ref[...].astype(f32)
    for j in range(ways(rows)):
        spread[:, j * width : (j + 1) * width] = jnp.where(block == j, returned, 0.0).astype(bf16)
    unused, place = fold(req, rows)
    part = rows // ways(rows)
    step = part
    for first in range(0, part, step):
        spot = lax.broadcasted_iota(jnp.int32, (step, LANES), 0) + first
        hot = jnp.concatenate(
            [one_hot(place[i : i + 1, :] == spot) for i in range(lists)], axis=1
        )
        sums = jnp.dot(hot, spread[...], preferred_element_type=f32)
        for j in range(ways(rows)):
            at = slice(j * part + first, j * part + first + step)
            new_ref[at, :], m_new_ref[at, :], v_new_ref[at, :] = adam_update(
                table_ref[at, :],
                m_ref[at, :],
                v_ref[at, :],
                sums[:, j * width : (j + 1) * width] * scale,
            )


def place_kernel(dims, plan, digits_ref, *refs):
    sources = refs[: len(plan)]
    out, hot_out, hot_rows, sems = refs[-4:]
    shard = sources[0].shape[-2]
    half = out.shape[1] // 2
    copies = []
    hots = 0
    for ref, (cols, main, k, core) in zip(sources, plan):
        other = 3 - main
        for i in range(ref.shape[0]):
            for j in range(ref.shape[1]):
                turn = {0: j, main: k, other: i}
                digit = [
                    lax.rem(digits_ref[level] - turn[level] + dims[level], dims[level])
                    for level in range(3)
                ]
                chip = (digit[0] * dims[1] + digit[1]) * dims[2] + digit[2]
                side = lax.rem(digits_ref[3] + core, 2)
                row = pl.multiple_of((chip * 2 + side) * shard, shard)
                copies.append(
                    (ref.at[i, j, :, :half], out.at[pl.ds(row, shard), pl.ds(cols * half, half)])
                )
                if cols == 0:
                    hot_rows[hots] = ref[i, j, :, half:].astype(f32)
                    copies.append((hot_rows.at[hots], hot_out.at[pl.ds(row, shard), :]))
                    hots += 1
    for copy in start_copies(sems, copies):
        copy.wait()


def place(dims, plan, digits, sources, rank, devices, before):
    shard, split = sources[0].shape[-2:]
    rows = shard * devices
    before = list(before or ())
    hbm, vmem = pl.BlockSpec(memory_space=pl.ANY), pl.BlockSpec(memory_space=pltpu.VMEM)
    first = 1 + len(sources)
    blocks = [s.shape[0] * s.shape[1] for s in sources]
    hots = sum(b for b, p in zip(blocks, plan) if p[0] == 0)
    return pl.pallas_call(
        functools.partial(place_kernel, dims, tuple(plan)),
        out_shape=[
            jax.ShapeDtypeStruct((rows, 2 * rank), bf16),
            jax.ShapeDtypeStruct((rows, split - rank), f32),
        ],
        in_specs=[pl.BlockSpec(memory_space=pltpu.SMEM)]
        + [vmem] * len(sources)
        + [hbm] * len(before),
        out_specs=[hbm, hbm],
        input_output_aliases={first + i: i for i in range(len(before))},
        scratch_shapes=[
            pltpu.VMEM((hots, shard, split - rank), f32),
            pltpu.SemaphoreType.DMA((sum(blocks) + hots,)),
        ],
        compiler_params=pltpu.CompilerParams(vmem_limit_bytes=24 << 20),
        cost_estimate=pl.CostEstimate(
            flops=0, bytes_accessed=4 * rows * rank, transcendentals=0
        ),
        name="place",
    )(digits, *sources, *before)


def split_levels(devices):
    cores = 2 if devices % 2 == 0 else 1
    chips = devices // cores
    bits = chips.bit_length() - 1
    if chips != 1 << bits:
        return (chips, 1, 1, cores)
    low = bits // 3
    mid = (bits - low) // 2
    return (1 << (bits - low - mid), 1 << mid, 1 << low, cores)


def body(
    sizes,
    cotangent,
    hot_table,
    cold_table,
    cold_m,
    cold_v,
    cross_down,
    cross_up,
    cross_bias,
    dense_master,
    dense_m,
    dense_v,
    hot_ids,
    lookup_slot,
    fetch_rows,
):
    devices = lax.axis_size("dev")
    sample_count, fields = hot_ids.shape
    slab_rows, emb_width = cold_table.shape
    hot_rows = hot_table.shape[0]
    capacity = fetch_rows.shape[2]
    cross_width, rank = cross_down.shape
    shard = dense_master.shape[0]
    scale_mean = 1.0 / devices
    slots = devices * capacity
    lookups = sample_count * fields
    dims = sizes[:3]
    SDS = jax.ShapeDtypeStruct

    me = lax.axis_index("dev")
    strides = [1] * 4
    for i in (2, 1, 0):
        strides[i] = strides[i + 1] * sizes[i + 1]
    digits = jnp.stack([(me // strides[i]) % sizes[i] for i in range(4)]).astype(jnp.int32)

    def exchange(value, level, k):
        size, stride = sizes[level], strides[level]
        pairs = []
        for d in range(devices):
            digit = (d // stride) % size
            pairs.append((d, d + ((digit + k) % size - digit) * stride))
        return lax.ppermute(value, "dev", pairs)

    def swap(value):
        return exchange(value, 3, 1) if sizes[3] == 2 else None

    def all_to_all(value):
        return lax.all_to_all(value, "dev", split_axis=0, concat_axis=0, tiled=True)

    folded = fold_table(cold_table)
    (hot_x0,) = call(
        hot_pick_kernel,
        [SDS((sample_count, cross_width), bf16)],
        [hot_ids, lookup_slot, hot_table],
        40 * lookups * hot_rows * emb_width,
        "hot_pick",
        scratch=[pltpu.VMEM((hot_rows // ways(hot_rows), ways(hot_rows) * emb_width), bf16)],
    )
    requests = all_to_all(fetch_rows.reshape(devices, 1, capacity))
    req = requests.reshape(slots // LANES, LANES)
    (picked,) = call(
        functools.partial(owner_pick_kernel, slab_rows),
        [SDS((slots, emb_width), bf16)],
        [requests, folded],
        4 * slots * slab_rows * emb_width,
        "owner_pick",
    )
    fetched = all_to_all(picked.reshape(devices, capacity, emb_width)).reshape(slots, emb_width)

    order_a, order_b = (2, 1, 0), (1, 2, 0)
    shape_a = tuple(dims[i] for i in order_a) + (shard, rank)
    shape_b = tuple(dims[i] for i in order_b) + (shard, rank)
    bias_part, keep_a, send_a, keep_b, send_b, grad_input = call(
        functools.partial(forward_kernel, dims, order_a, order_b),
        [
            SDS((fields, emb_width), f32),
            SDS(shape_a, bf16),
            SDS(shape_a, bf16),
            SDS(shape_b, bf16),
            SDS(shape_b, bf16),
            SDS((sample_count, cross_width), bf16),
        ],
        [
            digits,
            lookup_slot,
            fetched,
            cross_bias.reshape(1, cross_width),
            hot_x0,
            cotangent,
            cross_down,
            cross_up,
        ],
        4 * lookups * slots * emb_width,
        "forward",
        smem=(0,),
        hbm=(4, 5, 6, 7),
        out_hbm=(1, 2, 3, 4, 5),
        scratch=[
            pltpu.VMEM((sample_count, cross_width), bf16),
            pltpu.VMEM((sample_count, cross_width), bf16),
            pltpu.VMEM((slots // ways(slots), ways(slots) * emb_width), bf16),
            pltpu.VMEM((sample_count, cross_width), bf16),
            pltpu.VMEM((sample_count, cross_width), bf16),
            pltpu.VMEM(cross_down.shape, bf16),
            pltpu.VMEM(cross_up.shape, bf16),
            pltpu.VMEM(shape_a, bf16),
            pltpu.VMEM(shape_a, bf16),
            pltpu.VMEM(shape_b, bf16),
            pltpu.VMEM(shape_b, bf16),
            pltpu.VMEM((sample_count, cross_width), bf16),
            pltpu.SemaphoreType.DMA((8 + fields,)),
        ],
        vmem=VMEM_MOST,
    )
    got_a = swap(send_a)
    got_b = swap(send_b)
    own_hot = hot_rows // devices
    shape_hot = tuple(dims[i] for i in order_a) + (own_hot, emb_width)
    hot_index = jnp.where(lookup_slot < 0, hot_ids, -1)
    keep_hot, send_hot = call(
        functools.partial(hot_sums_kernel, dims, order_a),
        [SDS(shape_hot, bf16), SDS(shape_hot, bf16)],
        [digits, hot_index, hot_index.T, grad_input],
        4 * lookups * hot_rows * emb_width,
        "hot_sums",
        smem=(0,),
        scratch=[pltpu.VMEM((lookups, ways(hot_rows) * emb_width), bf16)],
        vmem=VMEM_MOST,
    )
    got_hot = swap(send_hot)

    def add(terms, *at):
        return functools.reduce(
            lambda s, t: s + t, [t[skip + at].astype(f32) for t, skip in terms]
        )

    def pack(groups, *at):
        return jnp.concatenate([add(terms, *at) for terms in groups], axis=-1)

    def step_sends(groups, level):
        return [pack(groups, k).astype(bf16) for k in range(1, sizes[level])]

    def step_takes(groups, level, sends):
        later = [[(t, skip + (0,)) for t, skip in terms] for terms in groups]
        for k, send in enumerate(sends):
            got = exchange(send, level, k + 1)
            start = 0
            for terms, old in zip(later, groups):
                wide = old[0][0].shape[-1]
                terms.append((got[..., start : start + wide], ()))
                start += wide
        return later

    groups_b = [[(keep_b, ()), (got_b, ())]]
    groups_a = [[(keep_a, ()), (got_a, ())], [(keep_hot, ()), (got_hot, ())]]
    sends_b = step_sends(groups_b, order_b[0])
    sends_a = step_sends(groups_a, order_a[0])
    grad_input, sends_a, sends_b = lax.optimization_barrier((grad_input, sends_a, sends_b))
    groups_b = step_takes(groups_b, order_b[0], sends_b)
    groups_a = step_takes(groups_a, order_a[0], sends_a)
    whole = capacity % 16 == 0
    (parcel,) = call(
        cold_sums_kernel,
        [
            SDS(
                (devices, capacity + fields, emb_width) if whole else (1, slots + fields, emb_width),
                bf16,
            )
        ],
        [lookup_slot, lookup_slot.T, grad_input, bias_part],
        4 * lookups * slots * emb_width,
        "cold_sums",
        scratch=[pltpu.VMEM((lookups, ways(slots) * emb_width), bf16)],
        vmem=VMEM_MOST,
    )
    if not whole:
        parcel = jnp.concatenate(
            [
                parcel[0, :slots].reshape(devices, capacity, emb_width),
                jnp.broadcast_to(parcel[:, slots:], (devices, fields, emb_width)),
            ],
            axis=1,
        )
    arrived = all_to_all(parcel)
    groups_b = step_takes(groups_b, order_b[1], step_sends(groups_b, order_b[1]))
    groups_a = step_takes(groups_a, order_a[1], step_sends(groups_a, order_a[1]))
    groups = [groups_a[0], groups_b[0], groups_a[1]]
    sums = [pack(groups, k) for k in range(sizes[0])]

    returned = arrived[:, :capacity].reshape(slots, emb_width)
    like = SDS(cold_table.shape, f32)
    cold_new, cold_m_new, cold_v_new = call(
        functools.partial(cold_adam_kernel, scale_mean),
        [like] * 3,
        [req, returned, cold_table, cold_m, cold_v],
        4 * slots * slab_rows * emb_width,
        "cold_adam",
        scratch=[pltpu.VMEM((slots, ways(slab_rows) * emb_width), bf16)],
    )
    bias_grad = (
        jnp.sum(arrived[:, capacity:].astype(f32), axis=0) * scale_mean
    ).reshape(cross_width)

    later = [exchange(sums[k].astype(bf16), 0, k) for k in range(1, sizes[0])]
    later, cold_new, cold_m_new, cold_v_new, bias_grad = lax.optimization_barrier(
        (later, cold_new, cold_m_new, cold_v_new, bias_grad)
    )
    dense_own = sums[0]
    for got in later:
        dense_own = dense_own + got.astype(f32)

    master_new, dense_m_new, dense_v_new = adam_update(
        dense_master, dense_m, dense_v, dense_own[:, : 2 * rank] * scale_mean
    )
    weights = jnp.concatenate(
        [master_new[:, :rank], dense_own[:, 2 * rank :] * scale_mean, master_new[:, rank:]], axis=1
    ).astype(bf16)
    split = rank + emb_width
    along_z = [weights] + [exchange(weights, 0, k) for k in range(1, sizes[0])]
    plan, got = [], []
    for cols, (level, main) in enumerate(((1, 2), (2, 1))):
        block = jnp.stack([w[:, split:] if cols else w[:, :split] for w in along_z])
        block = jnp.stack(
            [block] + [exchange(block, level, k) for k in range(1, sizes[level])]
        )
        for k in range(sizes[main]):
            plan.append((cols, main, k))
            got.append(exchange(block, main, k) if k else block)

    def put(which, core, values, before):
        return place(
            dims, [plan[i] + (core,) for i in which], digits, values, rank, devices, before
        )

    near = [i for i, p in enumerate(plan) if p[2] == 0]
    far = [i for i, p in enumerate(plan) if p[2] > 0]
    outs = put(near, 0, [got[i] for i in near], None)
    outs = put(near, 1, [swap(got[i]) for i in near], outs)
    if far:
        values, outs = lax.optimization_barrier(([got[i] for i in far], outs))
        others = [swap(v) for v in values]
        outs = put(far, 0, values, outs)
        outs = put(far, 1, others, outs)
    new_weights, hot_grad = outs
    return (
        hot_grad,
        bias_grad,
        cold_new,
        cold_m_new,
        cold_v_new,
        master_new,
        dense_m_new,
        dense_v_new,
        new_weights,
    )


def solution(mesh):
    sizes = split_levels(mesh.shape["dev"])
    return jax.shard_map(
        functools.partial(body, sizes),
        mesh=mesh,
        in_specs=(
            P("dev", None),
            P(),
            P("dev", None),
            P("dev", None),
            P("dev", None),
            P(),
            P(),
            P(),
            P("dev", None),
            P("dev", None),
            P("dev", None),
            P("dev", None),
            P("dev", None),
            P("dev", None, None),
        ),
        out_specs=(
            P(),
            P(),
            P("dev", None),
            P("dev", None),
            P("dev", None),
            P("dev", None),
            P("dev", None),
            P("dev", None),
            P(),
        ),
        check_vma=False,
    )
```

```python
import functools

import jax
import jax.numpy as jnp
from jax import lax
from jax.experimental import pallas as pl
from jax.experimental.pallas import tpu as pltpu
from jax.sharding import PartitionSpec as P

first_decay = 0.9
second_decay = 0.999
adam_epsilon = 1e-08
learn_rate = 0.01
first_fix = 1.0 - (0.9**10) ** 10
second_fix = 1.0 - (0.999**10) ** 10

LANES = 128
VMEM_MOST = 48 << 20
f32 = jnp.float32
bf16 = jnp.bfloat16


def adam_update(params, moment_one, moment_two, gradient):
    moment_one = first_decay * moment_one + (1.0 - first_decay) * gradient
    moment_two = second_decay * moment_two + (1.0 - second_decay) * gradient * gradient
    params = params - learn_rate * (moment_one / first_fix) / (
        jnp.sqrt(moment_two / second_fix) + adam_epsilon
    )
    return (params, moment_one, moment_two)


def call(kernel, outs, args, flops, name, smem=(), hbm=(), out_hbm=(), scratch=(), vmem=24 << 20):
    specs = [
        pl.BlockSpec(
            memory_space=pltpu.SMEM if i in smem else pl.ANY if i in hbm else pltpu.VMEM
        )
        for i in range(len(args))
    ]
    moved = sum(a.size * a.dtype.itemsize for a in list(args) + list(outs))
    return pl.pallas_call(
        kernel,
        out_shape=outs,
        in_specs=specs,
        out_specs=[
            pl.BlockSpec(memory_space=pl.ANY if i in out_hbm else pltpu.VMEM)
            for i in range(len(outs))
        ],
        scratch_shapes=list(scratch),
        compiler_params=pltpu.CompilerParams(vmem_limit_bytes=vmem),
        cost_estimate=pl.CostEstimate(flops=flops, bytes_accessed=moved, transcendentals=0),
        name=name,
    )(*args)


def one_hot(mask):
    return jnp.where(mask, 1.0, 0.0).astype(bf16)


def ways(rows):
    return 4 if rows % 64 == 0 else 1


def fold(index, rows):
    part = rows // ways(rows)
    block = jnp.zeros_like(index)
    for j in range(1, ways(rows)):
        block = block + jnp.where(index >= j * part, 1, 0)
    return block, index - block * part


def lay_beside(table, out_ref):
    rows, width = table.shape
    part = rows // ways(rows)
    for j in range(ways(rows)):
        out_ref[:, j * width : (j + 1) * width] = table[j * part : (j + 1) * part].astype(bf16)


def pick_rows(block, place, folded, width):
    part = folded.shape[0]
    hot = one_hot(place == lax.broadcasted_iota(jnp.int32, (place.shape[0], part), 1))
    both = jnp.dot(hot, folded[...], preferred_element_type=f32)
    out = both[:, :width]
    for j in range(1, both.shape[1] // width):
        out = jnp.where(block == j, both[:, j * width : (j + 1) * width], out)
    return out


def stacked(columns, first, count):
    return jnp.concatenate([columns[:, f : f + 1] for f in range(first, first + count)], axis=0)


def columns_of(lists):
    turned = jnp.transpose(lists)
    return jnp.concatenate([turned[:, i : i + 1] for i in range(lists.shape[0])], axis=0)


def fold_table_kernel(table_ref, out_ref):
    lay_beside(table_ref[...], out_ref)


def fold_table(table):
    rows, width = table.shape
    return call(
        fold_table_kernel,
        [jax.ShapeDtypeStruct((rows // ways(rows), ways(rows) * width), bf16)],
        [table],
        0,
        "fold_table",
    )[0]


def owner_pick_kernel(rows, req_ref, folded_ref, out_ref):
    slots, width = out_ref.shape
    column = columns_of(req_ref[:, 0, :])
    block, place = fold(column, rows)
    step = 1024 if slots % 1024 == 0 else slots
    for first in range(0, slots, step):
        at = slice(first, first + step)
        out_ref[at, :] = pick_rows(block[at], place[at], folded_ref, width).astype(bf16)


def hot_pick_kernel(ids_ref, slot_ref, table_ref, out_ref, folded):
    samples, fields = ids_ref.shape
    rows, width = table_ref.shape
    lay_beside(table_ref[...], folded)
    block, place = fold(jnp.where(slot_ref[...] < 0, ids_ref[...], -1), rows)
    for f in range(fields):
        out_ref[:, f * width : (f + 1) * width] = pick_rows(
            block[:, f : f + 1], place[:, f : f + 1], folded, width
        ).astype(bf16)


def store_halves(digits_ref, dims, order, sums, first, keep_ref, send_ref):
    shard = keep_ref.shape[-2]
    side = digits_ref[3]
    for j in range(sums.shape[0] // (2 * shard)):
        one = sums[2 * j * shard : (2 * j + 1) * shard]
        two = sums[(2 * j + 1) * shard : (2 * j + 2) * shard]
        chip = first // (2 * shard) + j
        digit = (chip // (dims[1] * dims[2]), chip // dims[2] % dims[1], chip % dims[2])
        at = tuple(
            lax.rem(digit[level] - digits_ref[level] + dims[level], dims[level])
            for level in order
        )
        keep_ref[at] = jnp.where(side == 0, one, two).astype(bf16)
        send_ref[at] = jnp.where(side == 0, two, one).astype(bf16)


def outer_sums(digits_ref, dims, order, left, right, keep_ref, send_ref):
    block = max(2 * keep_ref.shape[-2], min(left.shape[1], 1024))
    for first in range(0, left.shape[1], block):
        sums = lax.dot_general(
            left[:, first : first + block],
            right,
            (((0,), (0,)), ((), ())),
            preferred_element_type=f32,
        )
        store_halves(digits_ref, dims, order, sums, first, keep_ref, send_ref)


def start_copies(sems, pairs, first=0):
    copies = [
        pltpu.make_async_copy(source, target, sems.at[first + i])
        for i, (source, target) in enumerate(pairs)
    ]
    for copy in copies:
        copy.start()
    return copies


def forward_kernel(
    dims,
    order_a,
    order_b,
    digits_ref,
    slot_ref,
    fetched_ref,
    cross_bias_ref,
    hot_hbm,
    cot_hbm,
    down_hbm,
    up_hbm,
    bias_ref,
    keep_a_hbm,
    send_a_hbm,
    keep_b_hbm,
    send_b_hbm,
    grad_hbm,
    x0,
    gm,
    folded,
    hot_ref,
    cot_ref,
    down_ref,
    up_ref,
    keep_a,
    send_a,
    keep_b,
    send_b,
    grad_ref,
    sems,
):
    copies = start_copies(
        sems, ((hot_hbm, hot_ref), (cot_hbm, cot_ref), (up_hbm, up_ref), (down_hbm, down_ref))
    )
    samples, fields = slot_ref.shape
    slots, width = fetched_ref.shape
    lay_beside(fetched_ref[...], folded)
    block, place = fold(slot_ref[...], slots)
    group = 4 if fields % 4 == 0 else 1
    for first in range(0, fields, group):
        cold = pick_rows(
            stacked(block, first, group), stacked(place, first, group), folded, width
        )
        if first == 0:
            copies[0].wait()
            copies[1].wait()
        for i in range(group):
            f = first + i
            cols = slice(f * width, (f + 1) * width)
            picked = cold[i * samples : (i + 1) * samples] + hot_ref[:, cols].astype(f32)
            x0[:, cols] = picked.astype(bf16)
            mix = (cot_ref[:, cols].astype(f32) * picked).astype(bf16)
            gm[:, cols] = mix
            bias_ref[f : f + 1, :] = jnp.sum(mix.astype(f32), axis=0, keepdims=True)
    copies[2].wait()
    grad_latent = lax.dot_general(
        gm[...], up_ref[...], (((1,), (1,)), ((), ())), preferred_element_type=f32
    ).astype(bf16)
    outer_sums(digits_ref, dims, order_a, x0, grad_latent, keep_a, send_a)
    done = start_copies(sems, ((send_a, send_a_hbm), (keep_a, keep_a_hbm)), 4)
    copies[3].wait()
    latent = jnp.dot(x0[...], down_ref[...], preferred_element_type=f32).astype(bf16)
    outer_sums(digits_ref, dims, order_b, gm, latent, keep_b, send_b)
    done += start_copies(sems, ((send_b, send_b_hbm), (keep_b, keep_b_hbm)), 6)
    for first in range(0, fields, group):
        cols = slice(first * width, (first + group) * width)
        mixing = (
            jnp.dot(latent, up_ref[:, cols], preferred_element_type=f32) + cross_bias_ref[:, cols]
        )
        back = lax.dot_general(
            grad_latent, down_ref[cols, :], (((1,), (1,)), ((), ())), preferred_element_type=f32
        )
        grad = cot_ref[:, cols].astype(f32) * (mixing + 1.0) + back
        grad_ref[:, cols] = grad.astype(bf16)
        done += start_copies(
            sems, ((grad_ref.at[:, cols], grad_hbm.at[:, cols]),), 8 + first // group
        )
    for copy in done:
        copy.wait()


def add_up(lists, total, grads, use):
    fields, samples = lists.shape
    unused, place = fold(lists, total)
    part = total // ways(total)
    width = grads.shape[1] // ways(total)
    step = part
    for first in range(0, part, step):
        spot = lax.broadcasted_iota(jnp.int32, (step, samples), 0) + first
        hot = jnp.concatenate(
            [one_hot(place[f : f + 1, :] == spot) for f in range(fields)], axis=1
        )
        sums = jnp.dot(hot, grads[...], preferred_element_type=f32)
        for j in range(ways(total)):
            use(j * part + first, sums[:, j * width : (j + 1) * width])


def lay_by_block(block, grad, grads, rows):
    width = grad.shape[1]
    for j in range(grads.shape[1] // width):
        grads[rows, j * width : (j + 1) * width] = jnp.where(block == j, grad, 0.0).astype(bf16)


def lay_all_by_block(index, total, grad_ref, grads):
    samples, fields = index.shape
    width = grad_ref.shape[1] // fields
    block, unused = fold(index, total)
    for f in range(fields):
        lay_by_block(
            block[:, f : f + 1],
            grad_ref[:, f * width : (f + 1) * width].astype(f32),
            grads,
            slice(f * samples, (f + 1) * samples),
        )


def hot_sums_kernel(dims, order, digits_ref, id_ref, id_rows_ref, grad_ref, keep_ref, send_ref, grads):
    hot_rows = 2 * keep_ref.size // keep_ref.shape[-1]
    lay_all_by_block(id_ref[...], hot_rows, grad_ref, grads)

    def use(first, sums):
        store_halves(digits_ref, dims, order, sums, first, keep_ref, send_ref)

    add_up(id_rows_ref[...], hot_rows, grads, use)


def cold_sums_kernel(slot_ref, slot_rows_ref, grad_ref, bias_ref, cold_ref, grads):
    fields = slot_ref.shape[1]
    devices, capacity, width = cold_ref.shape
    capacity -= fields
    slots = devices * capacity
    lay_all_by_block(slot_ref[...], slots, grad_ref, grads)

    def use(first, sums):
        sums = sums.astype(bf16)
        at, end = first, first + sums.shape[0]
        while at < end:
            owner, slot = at // capacity, at % capacity
            count = min(capacity - slot, end - at)
            cold_ref[owner, slot : slot + count, :] = sums[at - first : at - first + count]
            at += count

    add_up(slot_rows_ref[...], slots, grads, use)
    bias = bias_ref[...].astype(bf16)
    for owner in range(devices):
        cold_ref[owner, capacity:, :] = bias


def cold_adam_kernel(
    scale, req_ref, ret_ref, table_ref, m_ref, v_ref, new_ref, m_new_ref, v_new_ref, spread
):
    lists = req_ref.shape[0]
    rows, width = table_ref.shape
    req = req_ref[...]
    block, unused = fold(columns_of(req), rows)
    returned = ret_ref[...].astype(f32)
    for j in range(ways(rows)):
        spread[:, j * width : (j + 1) * width] = jnp.where(block == j, returned, 0.0).astype(bf16)
    unused, place = fold(req, rows)
    part = rows // ways(rows)
    step = part
    for first in range(0, part, step):
        spot = lax.broadcasted_iota(jnp.int32, (step, LANES), 0) + first
        hot = jnp.concatenate(
            [one_hot(place[i : i + 1, :] == spot) for i in range(lists)], axis=1
        )
        sums = jnp.dot(hot, spread[...], preferred_element_type=f32)
        for j in range(ways(rows)):
            at = slice(j * part + first, j * part + first + step)
            new_ref[at, :], m_new_ref[at, :], v_new_ref[at, :] = adam_update(
                table_ref[at, :],
                m_ref[at, :],
                v_ref[at, :],
                sums[:, j * width : (j + 1) * width] * scale,
            )


def place_kernel(dims, plan, digits_ref, *refs):
    sources = refs[: len(plan)]
    out, hot_out, hot_rows, sems = refs[-4:]
    shard = sources[0].shape[-2]
    half = out.shape[1] // 2
    copies = []
    hots = 0
    for ref, (cols, main, k, core) in zip(sources, plan):
        other = 3 - main
        for i in range(ref.shape[0]):
            for j in range(ref.shape[1]):
                turn = {0: j, main: k, other: i}
                digit = [
                    lax.rem(digits_ref[level] - turn[level] + dims[level], dims[level])
                    for level in range(3)
                ]
                chip = (digit[0] * dims[1] + digit[1]) * dims[2] + digit[2]
                side = lax.rem(digits_ref[3] + core, 2)
                row = pl.multiple_of((chip * 2 + side) * shard, shard)
                copies.append(
                    (ref.at[i, j, :, :half], out.at[pl.ds(row, shard), pl.ds(cols * half, half)])
                )
                if cols == 0:
                    hot_rows[hots] = ref[i, j, :, half:].astype(f32)
                    copies.append((hot_rows.at[hots], hot_out.at[pl.ds(row, shard), :]))
                    hots += 1
    for copy in start_copies(sems, copies):
        copy.wait()


def place(dims, plan, digits, sources, rank, devices, before):
    shard, split = sources[0].shape[-2:]
    rows = shard * devices
    before = list(before or ())
    hbm, vmem = pl.BlockSpec(memory_space=pl.ANY), pl.BlockSpec(memory_space=pltpu.VMEM)
    first = 1 + len(sources)
    blocks = [s.shape[0] * s.shape[1] for s in sources]
    hots = sum(b for b, p in zip(blocks, plan) if p[0] == 0)
    return pl.pallas_call(
        functools.partial(place_kernel, dims, tuple(plan)),
        out_shape=[
            jax.ShapeDtypeStruct((rows, 2 * rank), bf16),
            jax.ShapeDtypeStruct((rows, split - rank), f32),
        ],
        in_specs=[pl.BlockSpec(memory_space=pltpu.SMEM)]
        + [vmem] * len(sources)
        + [hbm] * len(before),
        out_specs=[hbm, hbm],
        input_output_aliases={first + i: i for i in range(len(before))},
        scratch_shapes=[
            pltpu.VMEM((hots, shard, split - rank), f32),
            pltpu.SemaphoreType.DMA((sum(blocks) + hots,)),
        ],
        compiler_params=pltpu.CompilerParams(vmem_limit_bytes=24 << 20),
        cost_estimate=pl.CostEstimate(
            flops=0, bytes_accessed=4 * rows * rank, transcendentals=0
        ),
        name="place",
    )(digits, *sources, *before)


def split_levels(devices):
    cores = 2 if devices % 2 == 0 else 1
    chips = devices // cores
    bits = chips.bit_length() - 1
    if chips != 1 << bits:
        return (chips, 1, 1, cores)
    low = bits // 3
    mid = (bits - low) // 2
    return (1 << (bits - low - mid), 1 << mid, 1 << low, cores)


def body(
    sizes,
    cotangent,
    hot_table,
    cold_table,
    cold_m,
    cold_v,
    cross_down,
    cross_up,
    cross_bias,
    dense_master,
    dense_m,
    dense_v,
    hot_ids,
    lookup_slot,
    fetch_rows,
):
    devices = lax.axis_size("dev")
    sample_count, fields = hot_ids.shape
    slab_rows, emb_width = cold_table.shape
    hot_rows = hot_table.shape[0]
    capacity = fetch_rows.shape[2]
    cross_width, rank = cross_down.shape
    shard = dense_master.shape[0]
    scale_mean = 1.0 / devices
    slots = devices * capacity
    lookups = sample_count * fields
    dims = sizes[:3]
    SDS = jax.ShapeDtypeStruct

    me = lax.axis_index("dev")
    strides = [1] * 4
    for i in (2, 1, 0):
        strides[i] = strides[i + 1] * sizes[i + 1]
    digits = jnp.stack([(me // strides[i]) % sizes[i] for i in range(4)]).astype(jnp.int32)

    def exchange(value, level, k):
        size, stride = sizes[level], strides[level]
        pairs = []
        for d in range(devices):
            digit = (d // stride) % size
            pairs.append((d, d + ((digit + k) % size - digit) * stride))
        return lax.ppermute(value, "dev", pairs)

    def swap(value):
        return exchange(value, 3, 1) if sizes[3] == 2 else None

    def all_to_all(value):
        return lax.all_to_all(value, "dev", split_axis=0, concat_axis=0, tiled=True)

    folded = fold_table(cold_table)
    (hot_x0,) = call(
        hot_pick_kernel,
        [SDS((sample_count, cross_width), bf16)],
        [hot_ids, lookup_slot, hot_table],
        40 * lookups * hot_rows * emb_width,
        "hot_pick",
        scratch=[pltpu.VMEM((hot_rows // ways(hot_rows), ways(hot_rows) * emb_width), bf16)],
    )
    requests = all_to_all(fetch_rows.reshape(devices, 1, capacity))
    req = requests.reshape(slots // LANES, LANES)
    (picked,) = call(
        functools.partial(owner_pick_kernel, slab_rows),
        [SDS((slots, emb_width), bf16)],
        [requests, folded],
        4 * slots * slab_rows * emb_width,
        "owner_pick",
    )
    fetched = all_to_all(picked.reshape(devices, capacity, emb_width)).reshape(slots, emb_width)

    order_a, order_b = (2, 1, 0), (1, 2, 0)
    shape_a = tuple(dims[i] for i in order_a) + (shard, rank)
    shape_b = tuple(dims[i] for i in order_b) + (shard, rank)
    bias_part, keep_a, send_a, keep_b, send_b, grad_input = call(
        functools.partial(forward_kernel, dims, order_a, order_b),
        [
            SDS((fields, emb_width), f32),
            SDS(shape_a, bf16),
            SDS(shape_a, bf16),
            SDS(shape_b, bf16),
            SDS(shape_b, bf16),
            SDS((sample_count, cross_width), bf16),
        ],
        [
            digits,
            lookup_slot,
            fetched,
            cross_bias.reshape(1, cross_width),
            hot_x0,
            cotangent,
            cross_down,
            cross_up,
        ],
        4 * lookups * slots * emb_width,
        "forward",
        smem=(0,),
        hbm=(4, 5, 6, 7),
        out_hbm=(1, 2, 3, 4, 5),
        scratch=[
            pltpu.VMEM((sample_count, cross_width), bf16),
            pltpu.VMEM((sample_count, cross_width), bf16),
            pltpu.VMEM((slots // ways(slots), ways(slots) * emb_width), bf16),
            pltpu.VMEM((sample_count, cross_width), bf16),
            pltpu.VMEM((sample_count, cross_width), bf16),
            pltpu.VMEM(cross_down.shape, bf16),
            pltpu.VMEM(cross_up.shape, bf16),
            pltpu.VMEM(shape_a, bf16),
            pltpu.VMEM(shape_a, bf16),
            pltpu.VMEM(shape_b, bf16),
            pltpu.VMEM(shape_b, bf16),
            pltpu.VMEM((sample_count, cross_width), bf16),
            pltpu.SemaphoreType.DMA((8 + fields,)),
        ],
        vmem=VMEM_MOST,
    )
    got_a = swap(send_a)
    got_b = swap(send_b)
    own_hot = hot_rows // devices
    shape_hot = tuple(dims[i] for i in order_a) + (own_hot, emb_width)
    hot_index = jnp.where(lookup_slot < 0, hot_ids, -1)
    keep_hot, send_hot = call(
        functools.partial(hot_sums_kernel, dims, order_a),
        [SDS(shape_hot, bf16), SDS(shape_hot, bf16)],
        [digits, hot_index, hot_index.T, grad_input],
        4 * lookups * hot_rows * emb_width,
        "hot_sums",
        smem=(0,),
        scratch=[pltpu.VMEM((lookups, ways(hot_rows) * emb_width), bf16)],
        vmem=VMEM_MOST,
    )
    got_hot = swap(send_hot)

    def add(terms, *at):
        return functools.reduce(
            lambda s, t: s + t, [t[skip + at].astype(f32) for t, skip in terms]
        )

    def pack(groups, *at):
        return jnp.concatenate([add(terms, *at) for terms in groups], axis=-1)

    def step_sends(groups, level):
        return [pack(groups, k).astype(bf16) for k in range(1, sizes[level])]

    def step_takes(groups, level, sends):
        later = [[(t, skip + (0,)) for t, skip in terms] for terms in groups]
        for k, send in enumerate(sends):
            got = exchange(send, level, k + 1)
            start = 0
            for terms, old in zip(later, groups):
                wide = old[0][0].shape[-1]
                terms.append((got[..., start : start + wide], ()))
                start += wide
        return later

    groups_b = [[(keep_b, ()), (got_b, ())]]
    groups_a = [[(keep_a, ()), (got_a, ())], [(keep_hot, ()), (got_hot, ())]]
    sends_b = step_sends(groups_b, order_b[0])
    sends_b, got_hot = lax.optimization_barrier((sends_b, got_hot))
    groups_a[1] = [(keep_hot, ()), (got_hot, ())]
    sends_a = step_sends(groups_a, order_a[0])
    grad_input, sends_a, sends_b = lax.optimization_barrier((grad_input, sends_a, sends_b))
    groups_b = step_takes(groups_b, order_b[0], sends_b)
    groups_a = step_takes(groups_a, order_a[0], sends_a)
    whole = capacity % 16 == 0
    (parcel,) = call(
        cold_sums_kernel,
        [
            SDS(
                (devices, capacity + fields, emb_width) if whole else (1, slots + fields, emb_width),
                bf16,
            )
        ],
        [lookup_slot, lookup_slot.T, grad_input, bias_part],
        4 * lookups * slots * emb_width,
        "cold_sums",
        scratch=[pltpu.VMEM((lookups, ways(slots) * emb_width), bf16)],
        vmem=VMEM_MOST,
    )
    if not whole:
        parcel = jnp.concatenate(
            [
                parcel[0, :slots].reshape(devices, capacity, emb_width),
                jnp.broadcast_to(parcel[:, slots:], (devices, fields, emb_width)),
            ],
            axis=1,
        )
    arrived = all_to_all(parcel)
    groups_b = step_takes(groups_b, order_b[1], step_sends(groups_b, order_b[1]))
    groups_a = step_takes(groups_a, order_a[1], step_sends(groups_a, order_a[1]))
    groups = [groups_a[0], groups_b[0], groups_a[1]]
    sums = [pack(groups, k) for k in range(sizes[0])]

    returned = arrived[:, :capacity].reshape(slots, emb_width)
    like = SDS(cold_table.shape, f32)
    cold_new, cold_m_new, cold_v_new = call(
        functools.partial(cold_adam_kernel, scale_mean),
        [like] * 3,
        [req, returned, cold_table, cold_m, cold_v],
        4 * slots * slab_rows * emb_width,
        "cold_adam",
        scratch=[pltpu.VMEM((slots, ways(slab_rows) * emb_width), bf16)],
    )
    bias_grad = (
        jnp.sum(arrived[:, capacity:].astype(f32), axis=0) * scale_mean
    ).reshape(cross_width)

    later = [exchange(sums[k].astype(bf16), 0, k) for k in range(1, sizes[0])]
    later, cold_new, cold_m_new, cold_v_new, bias_grad = lax.optimization_barrier(
        (later, cold_new, cold_m_new, cold_v_new, bias_grad)
    )
    dense_own = sums[0]
    for got in later:
        dense_own = dense_own + got.astype(f32)

    master_new, dense_m_new, dense_v_new = adam_update(
        dense_master, dense_m, dense_v, dense_own[:, : 2 * rank] * scale_mean
    )
    weights = jnp.concatenate(
        [master_new[:, :rank], dense_own[:, 2 * rank :] * scale_mean, master_new[:, rank:]], axis=1
    ).astype(bf16)
    split = rank + emb_width
    along_z = [weights] + [exchange(weights, 0, k) for k in range(1, sizes[0])]
    plan, got = [], []
    for cols, (level, main) in enumerate(((1, 2), (2, 1))):
        block = jnp.stack([w[:, split:] if cols else w[:, :split] for w in along_z])
        block = jnp.stack(
            [block] + [exchange(block, level, k) for k in range(1, sizes[level])]
        )
        for k in range(sizes[main]):
            plan.append((cols, main, k))
            got.append(exchange(block, main, k) if k else block)

    def put(which, core, values, before):
        return place(
            dims, [plan[i] + (core,) for i in which], digits, values, rank, devices, before
        )

    near = [i for i, p in enumerate(plan) if p[2] == 0]
    far = [i for i, p in enumerate(plan) if p[2] > 0]
    outs = put(near, 0, [got[i] for i in near], None)
    outs = put(near, 1, [swap(got[i]) for i in near], outs)
    if far:
        values, outs = lax.optimization_barrier(([got[i] for i in far], outs))
        others = [swap(v) for v in values]
        outs = put(far, 0, values, outs)
        outs = put(far, 1, others, outs)
    new_weights, hot_grad = outs
    return (
        hot_grad,
        bias_grad,
        cold_new,
        cold_m_new,
        cold_v_new,
        master_new,
        dense_m_new,
        dense_v_new,
        new_weights,
    )


def solution(mesh):
    sizes = split_levels(mesh.shape["dev"])
    return jax.shard_map(
        functools.partial(body, sizes),
        mesh=mesh,
        in_specs=(
            P("dev", None),
            P(),
            P("dev", None),
            P("dev", None),
            P("dev", None),
            P(),
            P(),
            P(),
            P("dev", None),
            P("dev", None),
            P("dev", None),
            P("dev", None),
            P("dev", None),
            P("dev", None, None),
        ),
        out_specs=(
            P(),
            P(),
            P("dev", None),
            P("dev", None),
            P("dev", None),
            P("dev", None),
            P("dev", None),
            P("dev", None),
            P(),
        ),
        check_vma=False,
    )
```

```python
import functools

import jax
import jax.numpy as jnp
from jax import lax
from jax.experimental import pallas as pl
from jax.experimental.pallas import tpu as pltpu
from jax.sharding import PartitionSpec as P

first_decay = 0.9
second_decay = 0.999
adam_epsilon = 1e-08
learn_rate = 0.01
first_fix = 1.0 - (0.9**10) ** 10
second_fix = 1.0 - (0.999**10) ** 10

LANES = 128
VMEM_MOST = 48 << 20
f32 = jnp.float32
bf16 = jnp.bfloat16


def adam_update(params, moment_one, moment_two, gradient):
    moment_one = first_decay * moment_one + (1.0 - first_decay) * gradient
    moment_two = second_decay * moment_two + (1.0 - second_decay) * gradient * gradient
    params = params - learn_rate * (moment_one / first_fix) / (
        jnp.sqrt(moment_two / second_fix) + adam_epsilon
    )
    return (params, moment_one, moment_two)


def call(kernel, outs, args, flops, name, smem=(), hbm=(), out_hbm=(), scratch=(), vmem=24 << 20):
    specs = [
        pl.BlockSpec(
            memory_space=pltpu.SMEM if i in smem else pl.ANY if i in hbm else pltpu.VMEM
        )
        for i in range(len(args))
    ]
    moved = sum(a.size * a.dtype.itemsize for a in list(args) + list(outs))
    return pl.pallas_call(
        kernel,
        out_shape=outs,
        in_specs=specs,
        out_specs=[
            pl.BlockSpec(memory_space=pl.ANY if i in out_hbm else pltpu.VMEM)
            for i in range(len(outs))
        ],
        scratch_shapes=list(scratch),
        compiler_params=pltpu.CompilerParams(vmem_limit_bytes=vmem),
        cost_estimate=pl.CostEstimate(flops=flops, bytes_accessed=moved, transcendentals=0),
        name=name,
    )(*args)


def one_hot(mask):
    return jnp.where(mask, 1.0, 0.0).astype(bf16)


def ways(rows):
    return 4 if rows % 64 == 0 else 1


def fold(index, rows):
    part = rows // ways(rows)
    block = jnp.zeros_like(index)
    for j in range(1, ways(rows)):
        block = block + jnp.where(index >= j * part, 1, 0)
    return block, index - block * part


def lay_beside(table, out_ref):
    rows, width = table.shape
    part = rows // ways(rows)
    for j in range(ways(rows)):
        out_ref[:, j * width : (j + 1) * width] = table[j * part : (j + 1) * part].astype(bf16)


def pick_rows(block, place, folded, width):
    part = folded.shape[0]
    hot = one_hot(place == lax.broadcasted_iota(jnp.int32, (place.shape[0], part), 1))
    both = jnp.dot(hot, folded[...], preferred_element_type=f32)
    out = both[:, :width]
    for j in range(1, both.shape[1] // width):
        out = jnp.where(block == j, both[:, j * width : (j + 1) * width], out)
    return out


def stacked(columns, first, count):
    return jnp.concatenate([columns[:, f : f + 1] for f in range(first, first + count)], axis=0)


def columns_of(lists):
    turned = jnp.transpose(lists)
    return jnp.concatenate([turned[:, i : i + 1] for i in range(lists.shape[0])], axis=0)


def fold_table_kernel(table_ref, out_ref):
    lay_beside(table_ref[...], out_ref)


def fold_table(table):
    rows, width = table.shape
    return call(
        fold_table_kernel,
        [jax.ShapeDtypeStruct((rows // ways(rows), ways(rows) * width), bf16)],
        [table],
        0,
        "fold_table",
    )[0]


def owner_pick_kernel(rows, req_ref, folded_ref, out_ref):
    slots, width = out_ref.shape
    column = columns_of(req_ref[:, 0, :])
    block, place = fold(column, rows)
    step = 1024 if slots % 1024 == 0 else slots
    for first in range(0, slots, step):
        at = slice(first, first + step)
        out_ref[at, :] = pick_rows(block[at], place[at], folded_ref, width).astype(bf16)


def hot_pick_kernel(ids_ref, slot_ref, table_ref, out_ref, folded):
    samples, fields = ids_ref.shape
    rows, width = table_ref.shape
    lay_beside(table_ref[...], folded)
    block, place = fold(jnp.where(slot_ref[...] < 0, ids_ref[...], -1), rows)
    for f in range(fields):
        out_ref[:, f * width : (f + 1) * width] = pick_rows(
            block[:, f : f + 1], place[:, f : f + 1], folded, width
        ).astype(bf16)


def store_halves(digits_ref, dims, order, sums, first, keep_ref, send_ref):
    shard = keep_ref.shape[-2]
    side = digits_ref[3]
    for j in range(sums.shape[0] // (2 * shard)):
        one = sums[2 * j * shard : (2 * j + 1) * shard]
        two = sums[(2 * j + 1) * shard : (2 * j + 2) * shard]
        chip = first // (2 * shard) + j
        digit = (chip // (dims[1] * dims[2]), chip // dims[2] % dims[1], chip % dims[2])
        at = tuple(
            lax.rem(digit[level] - digits_ref[level] + dims[level], dims[level])
            for level in order
        )
        keep_ref[at] = jnp.where(side == 0, one, two).astype(bf16)
        send_ref[at] = jnp.where(side == 0, two, one).astype(bf16)


def outer_sums(digits_ref, dims, order, left, right, keep_ref, send_ref):
    block = max(2 * keep_ref.shape[-2], min(left.shape[1], 1024))
    for first in range(0, left.shape[1], block):
        sums = lax.dot_general(
            left[:, first : first + block],
            right,
            (((0,), (0,)), ((), ())),
            preferred_element_type=f32,
        )
        store_halves(digits_ref, dims, order, sums, first, keep_ref, send_ref)


def start_copies(sems, pairs, first=0):
    copies = [
        pltpu.make_async_copy(source, target, sems.at[first + i])
        for i, (source, target) in enumerate(pairs)
    ]
    for copy in copies:
        copy.start()
    return copies


def forward_kernel(
    dims,
    order_a,
    order_b,
    digits_ref,
    slot_ref,
    fetched_ref,
    cross_bias_ref,
    hot_hbm,
    cot_hbm,
    down_hbm,
    up_hbm,
    bias_ref,
    keep_a_hbm,
    send_a_hbm,
    keep_b_hbm,
    send_b_hbm,
    grad_hbm,
    x0,
    gm,
    folded,
    hot_ref,
    cot_ref,
    down_ref,
    up_ref,
    keep_a,
    send_a,
    keep_b,
    send_b,
    grad_ref,
    sems,
):
    copies = start_copies(
        sems, ((hot_hbm, hot_ref), (cot_hbm, cot_ref), (up_hbm, up_ref), (down_hbm, down_ref))
    )
    samples, fields = slot_ref.shape
    slots, width = fetched_ref.shape
    lay_beside(fetched_ref[...], folded)
    block, place = fold(slot_ref[...], slots)
    group = 4 if fields % 4 == 0 else 1
    for first in range(0, fields, group):
        cold = pick_rows(
            stacked(block, first, group), stacked(place, first, group), folded, width
        )
        if first == 0:
            copies[0].wait()
            copies[1].wait()
        for i in range(group):
            f = first + i
            cols = slice(f * width, (f + 1) * width)
            picked = cold[i * samples : (i + 1) * samples] + hot_ref[:, cols].astype(f32)
            x0[:, cols] = picked.astype(bf16)
            mix = (cot_ref[:, cols].astype(f32) * picked).astype(bf16)
            gm[:, cols] = mix
            bias_ref[f : f + 1, :] = jnp.sum(mix.astype(f32), axis=0, keepdims=True)
    copies[2].wait()
    grad_latent = lax.dot_general(
        gm[...], up_ref[...], (((1,), (1,)), ((), ())), preferred_element_type=f32
    ).astype(bf16)
    outer_sums(digits_ref, dims, order_a, x0, grad_latent, keep_a, send_a)
    done = start_copies(sems, ((send_a, send_a_hbm), (keep_a, keep_a_hbm)), 4)
    copies[3].wait()
    latent = jnp.dot(x0[...], down_ref[...], preferred_element_type=f32).astype(bf16)
    outer_sums(digits_ref, dims, order_b, gm, latent, keep_b, send_b)
    done += start_copies(sems, ((send_b, send_b_hbm), (keep_b, keep_b_hbm)), 6)
    for first in range(0, fields, group):
        cols = slice(first * width, (first + group) * width)
        mixing = (
            jnp.dot(latent, up_ref[:, cols], preferred_element_type=f32) + cross_bias_ref[:, cols]
        )
        back = lax.dot_general(
            grad_latent, down_ref[cols, :], (((1,), (1,)), ((), ())), preferred_element_type=f32
        )
        grad = cot_ref[:, cols].astype(f32) * (mixing + 1.0) + back
        grad_ref[:, cols] = grad.astype(bf16)
        done += start_copies(
            sems, ((grad_ref.at[:, cols], grad_hbm.at[:, cols]),), 8 + first // group
        )
    for copy in done:
        copy.wait()


def add_up(lists, total, grads, use):
    fields, samples = lists.shape
    unused, place = fold(lists, total)
    part = total // ways(total)
    width = grads.shape[1] // ways(total)
    step = part
    for first in range(0, part, step):
        spot = lax.broadcasted_iota(jnp.int32, (step, samples), 0) + first
        hot = jnp.concatenate(
            [one_hot(place[f : f + 1, :] == spot) for f in range(fields)], axis=1
        )
        sums = jnp.dot(hot, grads[...], preferred_element_type=f32)
        for j in range(ways(total)):
            use(j * part + first, sums[:, j * width : (j + 1) * width])


def lay_by_block(block, grad, grads, rows):
    width = grad.shape[1]
    for j in range(grads.shape[1] // width):
        grads[rows, j * width : (j + 1) * width] = jnp.where(block == j, grad, 0.0).astype(bf16)


def lay_all_by_block(index, total, grad_ref, grads):
    samples, fields = index.shape
    width = grad_ref.shape[1] // fields
    block, unused = fold(index, total)
    for f in range(fields):
        lay_by_block(
            block[:, f : f + 1],
            grad_ref[:, f * width : (f + 1) * width].astype(f32),
            grads,
            slice(f * samples, (f + 1) * samples),
        )


def hot_sums_kernel(dims, order, digits_ref, id_ref, id_rows_ref, grad_ref, keep_ref, send_ref, grads):
    hot_rows = 2 * keep_ref.size // keep_ref.shape[-1]
    lay_all_by_block(id_ref[...], hot_rows, grad_ref, grads)

    def use(first, sums):
        store_halves(digits_ref, dims, order, sums, first, keep_ref, send_ref)

    add_up(id_rows_ref[...], hot_rows, grads, use)


def cold_sums_kernel(slot_ref, slot_rows_ref, grad_ref, bias_ref, cold_ref, grads):
    fields = slot_ref.shape[1]
    devices, capacity, width = cold_ref.shape
    capacity -= fields
    slots = devices * capacity
    lay_all_by_block(slot_ref[...], slots, grad_ref, grads)

    def use(first, sums):
        sums = sums.astype(bf16)
        at, end = first, first + sums.shape[0]
        while at < end:
            owner, slot = at // capacity, at % capacity
            count = min(capacity - slot, end - at)
            cold_ref[owner, slot : slot + count, :] = sums[at - first : at - first + count]
            at += count

    add_up(slot_rows_ref[...], slots, grads, use)
    bias = bias_ref[...].astype(bf16)
    for owner in range(devices):
        cold_ref[owner, capacity:, :] = bias


def cold_adam_kernel(
    scale, req_ref, ret_ref, table_ref, m_ref, v_ref, new_ref, m_new_ref, v_new_ref, spread
):
    lists = req_ref.shape[0]
    rows, width = table_ref.shape
    req = req_ref[...]
    block, unused = fold(columns_of(req), rows)
    returned = ret_ref[...].astype(f32)
    for j in range(ways(rows)):
        spread[:, j * width : (j + 1) * width] = jnp.where(block == j, returned, 0.0).astype(bf16)
    unused, place = fold(req, rows)
    part = rows // ways(rows)
    step = part
    for first in range(0, part, step):
        spot = lax.broadcasted_iota(jnp.int32, (step, LANES), 0) + first
        hot = jnp.concatenate(
            [one_hot(place[i : i + 1, :] == spot) for i in range(lists)], axis=1
        )
        sums = jnp.dot(hot, spread[...], preferred_element_type=f32)
        for j in range(ways(rows)):
            at = slice(j * part + first, j * part + first + step)
            new_ref[at, :], m_new_ref[at, :], v_new_ref[at, :] = adam_update(
                table_ref[at, :],
                m_ref[at, :],
                v_ref[at, :],
                sums[:, j * width : (j + 1) * width] * scale,
            )


def place_kernel(dims, plan, digits_ref, *refs):
    sources = refs[: len(plan)]
    out, hot_out, hot_rows, sems = refs[-4:]
    shard = sources[0].shape[-2]
    half = out.shape[1] // 2
    copies = []
    hots = 0
    for ref, (cols, main, k, core) in zip(sources, plan):
        other = 3 - main
        for i in range(ref.shape[0]):
            for j in range(ref.shape[1]):
                turn = {0: j, main: k, other: i}
                digit = [
                    lax.rem(digits_ref[level] - turn[level] + dims[level], dims[level])
                    for level in range(3)
                ]
                chip = (digit[0] * dims[1] + digit[1]) * dims[2] + digit[2]
                side = lax.rem(digits_ref[3] + core, 2)
                row = pl.multiple_of((chip * 2 + side) * shard, shard)
                copies.append(
                    (ref.at[i, j, :, :half], out.at[pl.ds(row, shard), pl.ds(cols * half, half)])
                )
                if cols == 0:
                    hot_rows[hots] = ref[i, j, :, half:].astype(f32)
                    copies.append((hot_rows.at[hots], hot_out.at[pl.ds(row, shard), :]))
                    hots += 1
    for copy in start_copies(sems, copies):
        copy.wait()


def place(dims, plan, digits, sources, rank, devices, before):
    shard, split = sources[0].shape[-2:]
    rows = shard * devices
    before = list(before or ())
    hbm, vmem = pl.BlockSpec(memory_space=pl.ANY), pl.BlockSpec(memory_space=pltpu.VMEM)
    first = 1 + len(sources)
    blocks = [s.shape[0] * s.shape[1] for s in sources]
    hots = sum(b for b, p in zip(blocks, plan) if p[0] == 0)
    return pl.pallas_call(
        functools.partial(place_kernel, dims, tuple(plan)),
        out_shape=[
            jax.ShapeDtypeStruct((rows, 2 * rank), bf16),
            jax.ShapeDtypeStruct((rows, split - rank), f32),
        ],
        in_specs=[pl.BlockSpec(memory_space=pltpu.SMEM)]
        + [vmem] * len(sources)
        + [hbm] * len(before),
        out_specs=[hbm, hbm],
        input_output_aliases={first + i: i for i in range(len(before))},
        scratch_shapes=[
            pltpu.VMEM((hots, shard, split - rank), f32),
            pltpu.SemaphoreType.DMA((sum(blocks) + hots,)),
        ],
        compiler_params=pltpu.CompilerParams(vmem_limit_bytes=24 << 20),
        cost_estimate=pl.CostEstimate(
            flops=0, bytes_accessed=4 * rows * rank, transcendentals=0
        ),
        name="place",
    )(digits, *sources, *before)


def split_levels(devices):
    cores = 2 if devices % 2 == 0 else 1
    chips = devices // cores
    bits = chips.bit_length() - 1
    if chips != 1 << bits:
        return (chips, 1, 1, cores)
    low = bits // 3
    mid = (bits - low) // 2
    return (1 << (bits - low - mid), 1 << mid, 1 << low, cores)


def body(
    sizes,
    cotangent,
    hot_table,
    cold_table,
    cold_m,
    cold_v,
    cross_down,
    cross_up,
    cross_bias,
    dense_master,
    dense_m,
    dense_v,
    hot_ids,
    lookup_slot,
    fetch_rows,
):
    devices = lax.axis_size("dev")
    sample_count, fields = hot_ids.shape
    slab_rows, emb_width = cold_table.shape
    hot_rows = hot_table.shape[0]
    capacity = fetch_rows.shape[2]
    cross_width, rank = cross_down.shape
    shard = dense_master.shape[0]
    scale_mean = 1.0 / devices
    slots = devices * capacity
    lookups = sample_count * fields
    dims = sizes[:3]
    SDS = jax.ShapeDtypeStruct

    me = lax.axis_index("dev")
    strides = [1] * 4
    for i in (2, 1, 0):
        strides[i] = strides[i + 1] * sizes[i + 1]
    digits = jnp.stack([(me // strides[i]) % sizes[i] for i in range(4)]).astype(jnp.int32)

    def exchange(value, level, k):
        size, stride = sizes[level], strides[level]
        pairs = []
        for d in range(devices):
            digit = (d // stride) % size
            pairs.append((d, d + ((digit + k) % size - digit) * stride))
        return lax.ppermute(value, "dev", pairs)

    def swap(value):
        return exchange(value, 3, 1) if sizes[3] == 2 else None

    def all_to_all(value):
        return lax.all_to_all(value, "dev", split_axis=0, concat_axis=0, tiled=True)

    folded = fold_table(cold_table)
    (hot_x0,) = call(
        hot_pick_kernel,
        [SDS((sample_count, cross_width), bf16)],
        [hot_ids, lookup_slot, hot_table],
        40 * lookups * hot_rows * emb_width,
        "hot_pick",
        scratch=[pltpu.VMEM((hot_rows // ways(hot_rows), ways(hot_rows) * emb_width), bf16)],
    )
    requests = all_to_all(fetch_rows.reshape(devices, 1, capacity))
    req = requests.reshape(slots // LANES, LANES)
    (picked,) = call(
        functools.partial(owner_pick_kernel, slab_rows),
        [SDS((slots, emb_width), bf16)],
        [requests, folded],
        4 * slots * slab_rows * emb_width,
        "owner_pick",
    )
    fetched = all_to_all(picked.reshape(devices, capacity, emb_width)).reshape(slots, emb_width)

    order_a, order_b = (2, 1, 0), (1, 2, 0)
    shape_a = tuple(dims[i] for i in order_a) + (shard, rank)
    shape_b = tuple(dims[i] for i in order_b) + (shard, rank)
    bias_part, keep_a, send_a, keep_b, send_b, grad_input = call(
        functools.partial(forward_kernel, dims, order_a, order_b),
        [
            SDS((fields, emb_width), f32),
            SDS(shape_a, bf16),
            SDS(shape_a, bf16),
            SDS(shape_b, bf16),
            SDS(shape_b, bf16),
            SDS((sample_count, cross_width), bf16),
        ],
        [
            digits,
            lookup_slot,
            fetched,
            cross_bias.reshape(1, cross_width),
            hot_x0,
            cotangent,
            cross_down,
            cross_up,
        ],
        4 * lookups * slots * emb_width,
        "forward",
        smem=(0,),
        hbm=(4, 5, 6, 7),
        out_hbm=(1, 2, 3, 4, 5),
        scratch=[
            pltpu.VMEM((sample_count, cross_width), bf16),
            pltpu.VMEM((sample_count, cross_width), bf16),
            pltpu.VMEM((slots // ways(slots), ways(slots) * emb_width), bf16),
            pltpu.VMEM((sample_count, cross_width), bf16),
            pltpu.VMEM((sample_count, cross_width), bf16),
            pltpu.VMEM(cross_down.shape, bf16),
            pltpu.VMEM(cross_up.shape, bf16),
            pltpu.VMEM(shape_a, bf16),
            pltpu.VMEM(shape_a, bf16),
            pltpu.VMEM(shape_b, bf16),
            pltpu.VMEM(shape_b, bf16),
            pltpu.VMEM((sample_count, cross_width), bf16),
            pltpu.SemaphoreType.DMA((8 + fields,)),
        ],
        vmem=VMEM_MOST,
    )
    got_a = swap(send_a)
    got_b = swap(send_b)
    own_hot = hot_rows // devices
    shape_hot = tuple(dims[i] for i in order_a) + (own_hot, emb_width)
    hot_index = jnp.where(lookup_slot < 0, hot_ids, -1)
    keep_hot, send_hot = call(
        functools.partial(hot_sums_kernel, dims, order_a),
        [SDS(shape_hot, bf16), SDS(shape_hot, bf16)],
        [digits, hot_index, hot_index.T, grad_input],
        4 * lookups * hot_rows * emb_width,
        "hot_sums",
        smem=(0,),
        scratch=[pltpu.VMEM((lookups, ways(hot_rows) * emb_width), bf16)],
        vmem=VMEM_MOST,
    )
    got_hot = swap(send_hot)

    def add(terms, *at):
        return functools.reduce(
            lambda s, t: s + t, [t[skip + at].astype(f32) for t, skip in terms]
        )

    def pack(groups, *at):
        return jnp.concatenate([add(terms, *at) for terms in groups], axis=-1)

    def step_sends(groups, level):
        return [pack(groups, k).astype(bf16) for k in range(1, sizes[level])]

    def step_takes(groups, level, sends):
        later = [[(t, skip + (0,)) for t, skip in terms] for terms in groups]
        for k, send in enumerate(sends):
            got = exchange(send, level, k + 1)
            start = 0
            for terms, old in zip(later, groups):
                wide = old[0][0].shape[-1]
                terms.append((got[..., start : start + wide], ()))
                start += wide
        return later

    groups_b = [[(keep_b, ()), (got_b, ())]]
    groups_a = [[(keep_a, ()), (got_a, ())], [(keep_hot, ()), (got_hot, ())]]
    sends_b = step_sends(groups_b, order_b[0])
    sends_b, got_hot = lax.optimization_barrier((sends_b, got_hot))
    groups_a[1] = [(keep_hot, ()), (got_hot, ())]
    sends_a = step_sends(groups_a, order_a[0])
    grad_input, sends_a, sends_b = lax.optimization_barrier((grad_input, sends_a, sends_b))
    groups_a = step_takes(groups_a, order_a[0], sends_a)
    groups_b = step_takes(groups_b, order_b[0], sends_b)
    whole = capacity % 16 == 0
    (parcel,) = call(
        cold_sums_kernel,
        [
            SDS(
                (devices, capacity + fields, emb_width) if whole else (1, slots + fields, emb_width),
                bf16,
            )
        ],
        [lookup_slot, lookup_slot.T, grad_input, bias_part],
        4 * lookups * slots * emb_width,
        "cold_sums",
        scratch=[pltpu.VMEM((lookups, ways(slots) * emb_width), bf16)],
        vmem=VMEM_MOST,
    )
    if not whole:
        parcel = jnp.concatenate(
            [
                parcel[0, :slots].reshape(devices, capacity, emb_width),
                jnp.broadcast_to(parcel[:, slots:], (devices, fields, emb_width)),
            ],
            axis=1,
        )
    arrived = all_to_all(parcel)
    groups_b = step_takes(groups_b, order_b[1], step_sends(groups_b, order_b[1]))
    groups_a = step_takes(groups_a, order_a[1], step_sends(groups_a, order_a[1]))
    groups = [groups_a[0], groups_b[0], groups_a[1]]
    sums = [pack(groups, k) for k in range(sizes[0])]

    returned = arrived[:, :capacity].reshape(slots, emb_width)
    like = SDS(cold_table.shape, f32)
    cold_new, cold_m_new, cold_v_new = call(
        functools.partial(cold_adam_kernel, scale_mean),
        [like] * 3,
        [req, returned, cold_table, cold_m, cold_v],
        4 * slots * slab_rows * emb_width,
        "cold_adam",
        scratch=[pltpu.VMEM((slots, ways(slab_rows) * emb_width), bf16)],
    )
    bias_grad = (
        jnp.sum(arrived[:, capacity:].astype(f32), axis=0) * scale_mean
    ).reshape(cross_width)

    later = [exchange(sums[k].astype(bf16), 0, k) for k in range(1, sizes[0])]
    later[-1], cold_new, cold_m_new, cold_v_new, bias_grad = lax.optimization_barrier(
        (later[-1], cold_new, cold_m_new, cold_v_new, bias_grad)
    )
    dense_own = sums[0]
    for got in later:
        dense_own = dense_own + got.astype(f32)

    master_new, dense_m_new, dense_v_new = adam_update(
        dense_master, dense_m, dense_v, dense_own[:, : 2 * rank] * scale_mean
    )
    weights = jnp.concatenate(
        [master_new[:, :rank], dense_own[:, 2 * rank :] * scale_mean, master_new[:, rank:]], axis=1
    ).astype(bf16)
    split = rank + emb_width
    along_z = [weights] + [exchange(weights, 0, k) for k in range(1, sizes[0])]
    plan, got = [], []
    for cols, (level, main) in enumerate(((1, 2), (2, 1))):
        block = jnp.stack([w[:, split:] if cols else w[:, :split] for w in along_z])
        block = jnp.stack(
            [block] + [exchange(block, level, k) for k in range(1, sizes[level])]
        )
        for k in range(sizes[main]):
            plan.append((cols, main, k))
            got.append(exchange(block, main, k) if k else block)

    def put(which, core, values, before):
        return place(
            dims, [plan[i] + (core,) for i in which], digits, values, rank, devices, before
        )

    near = [i for i, p in enumerate(plan) if p[2] == 0]
    far = [i for i, p in enumerate(plan) if p[2] > 0]
    outs = put(near, 0, [got[i] for i in near], None)
    outs = put(near, 1, [swap(got[i]) for i in near], outs)
    if far:
        values, outs = lax.optimization_barrier(([got[i] for i in far], outs))
        others = [swap(v) for v in values]
        outs = put(far, 0, values, outs)
        outs = put(far, 1, others, outs)
    new_weights, hot_grad = outs
    return (
        hot_grad,
        bias_grad,
        cold_new,
        cold_m_new,
        cold_v_new,
        master_new,
        dense_m_new,
        dense_v_new,
        new_weights,
    )


def solution(mesh):
    sizes = split_levels(mesh.shape["dev"])
    return jax.shard_map(
        functools.partial(body, sizes),
        mesh=mesh,
        in_specs=(
            P("dev", None),
            P(),
            P("dev", None),
            P("dev", None),
            P("dev", None),
            P(),
            P(),
            P(),
            P("dev", None),
            P("dev", None),
            P("dev", None),
            P("dev", None),
            P("dev", None),
            P("dev", None, None),
        ),
        out_specs=(
            P(),
            P(),
            P("dev", None),
            P("dev", None),
            P("dev", None),
            P("dev", None),
            P("dev", None),
            P("dev", None),
            P(),
        ),
        check_vma=False,
    )
```
